256 devices in a mesh: rep: 16 (over y, z_lo), tp: 16 (over z_hi, x, core).
Axes of the slice: x: 4, y: 4, z: 8 (z_hi: 2, z_lo: 4; z = z_hi * 4 + z_lo), core: 2. Of those that a mesh axis runs over, the one named last changes fastest.
Arguments:
- hidden: bfloat16 [4, 256, 8192], P(None, ('rep', 'tp')), may hold values from -6 to 6
- w_query: bfloat16 [8192, 8192], P(None, 'tp'), may hold values from -0.0625 to 0.0625
- w_key: bfloat16 [8192, 512], P(None, 'tp'), may hold values from -0.1875 to 0.1875
- w_value: bfloat16 [8192, 512], P(None, 'tp'), may hold values from -0.0625 to 0.0625
- a_factors: bfloat16 [3, 8192, 64], P(None, 'rep'), may hold values from -0.0625 to 0.0625
- b_query: bfloat16 [64, 8192], P('rep', 'tp'), may hold values from -0.75 to 0.75
- b_key: bfloat16 [64, 512], P('rep', 'tp'), may hold values from -2 to 2
- b_value: bfloat16 [64, 512], P('rep', 'tp'), may hold values from -0.75 to 0.75
- key_cache: bfloat16 [256, 1536, 512], P(('rep', 'tp'))
- value_cache: bfloat16 [256, 1536, 512], P(('rep', 'tp')), may hold values from -6 to 6
- lengths: int32 [256], P(('rep', 'tp')), may hold values from 512 to 1536, as said below
Outputs:
- attended: bfloat16 [4, 256, 8192], P(None, 'rep', 'tp')
- new_keys: bfloat16 [4, 256, 512], P(None, ('rep', 'tp'))
- new_values: bfloat16 [4, 256, 512], P(None, ('rep', 'tp'))
The draws below stay inside these ranges and needn't reach their ends.
Inputs may be any that keep to these rules, and one draw needn't show every extreme that they name: Row r has its keys and values in slots 0 to lengths[r] - 1; some row has 1536 and some row 512.
All inputs are finite; a program needn't handle non-finite values.
Results may differ from the reference program's by a relative error of at most 0.0085.
The reference program's roundings to bfloat16 on the way count: a program that leaves them out, or rounds other values in their place, can miss the bound.
Values may be sent and summed in bfloat16 or wider, within the bound.
A program may use at most 128 MiB of HBM per device.

```python
import math
import jax
import jax.numpy as jnp
from jax import lax

D = 8192
HEADS = 64
KV_HEADS = 4
HEAD_DIM = 128
RANK = 64
CACHE_SLOTS = 1536
STEPS = 4
QW = 8192
KVW = 512
ROLLOUT_ROWS = 256


def draw_key_cache(key, part):
    key = jax.random.fold_in(key, 11)
    base_weight_key = jax.random.fold_in(key, 0)
    base_weights = jax.random.normal(base_weight_key, (ROLLOUT_ROWS, CACHE_SLOTS, KVW), jnp.float32) * 2.5
    return jnp.clip(base_weights, -15.0, 15.0).astype(jnp.bfloat16)


def draw_lengths(key, part):
    key = jax.random.fold_in(key, 5)
    drawn_key, longest_key, other_key = jax.random.split(key, 3)
    shortest = CACHE_SLOTS // 3
    drawn = jax.random.randint(drawn_key, (ROLLOUT_ROWS,), shortest, CACHE_SLOTS + 1)
    longest_at = jax.random.randint(longest_key, (), 0, ROLLOUT_ROWS)
    shortest_at = (longest_at + jax.random.randint(other_key, (), 1, ROLLOUT_ROWS)) % ROLLOUT_ROWS
    drawn = drawn.at[shortest_at].set(shortest)
    drawn = drawn.at[longest_at].set(CACHE_SLOTS)
    return drawn.astype(jnp.int32)


def shard_levels(rng, dims, cuts, least, top_value):
    def one(axis_at, shards_of):
        draws = jax.random.uniform(jax.random.fold_in(jax.random.fold_in(rng, 6), axis_at), (shards_of,), jnp.float32, least / len(cuts), top_value / len(cuts))
        return jnp.repeat(jnp.exp(draws), dims[axis_at] // shards_of).reshape((-1,) + (1,) * (len(dims) - axis_at - 1))

    level = one(*cuts[0])
    for cut in cuts[1:]:
        level = level * one(*cut)
    return level


def centred(key, shape, deviation, limit, pieces=(), held_as=jnp.bfloat16):
    entries = deviation * jax.random.normal(key, shape, jnp.float32)
    if pieces:
        entries = entries * shard_levels(key, shape, pieces, -0.22, 0.18)
    return jnp.clip(entries, -limit, limit).astype(held_as)


def setup_inputs(seed: int = 0) -> dict:
    keys = jax.random.split(jax.random.key(seed), 12)
    return {
        "hidden": centred(keys[0], (STEPS, ROLLOUT_ROWS, D), 1.0, 6.0, ((1, 256),)),
        "w_query": centred(keys[1], (D, QW), D ** -0.5, 0.0625, ((1, 16),)),
        "w_key": centred(keys[2], (D, KVW), (D // 8) ** -0.5, 0.1875, ((1, 16),)),
        "w_value": centred(keys[3], (D, KVW), D ** -0.5, 0.0625, ((1, 16),)),
        "a_factors": centred(keys[4], (3, D, RANK), D ** -0.5, 0.0625, ((1, 16),)),
        "b_query": centred(keys[5], (RANK, QW), RANK ** -0.5, 0.75, ((0, 16), (1, 16))),
        "b_key": centred(keys[6], (RANK, KVW), (RANK // 8) ** -0.5, 2.0, ((0, 16), (1, 16))),
        "b_value": centred(keys[7], (RANK, KVW), RANK ** -0.5, 0.75, ((0, 16), (1, 16))),
        "key_cache": draw_key_cache(jax.random.fold_in(keys[11], 71), 0),
        "value_cache": centred(keys[9], (ROLLOUT_ROWS, CACHE_SLOTS, KVW), 1.0, 6.0, ((0, 256),)),
        "lengths": draw_lengths(jax.random.fold_in(keys[11], 71), 0),
    }


THETA = 500000.0
SCALE = 0.5

def rotate(values, positions):
    half_dim = values.shape[-1] // 2
    frequency = THETA ** (-(jnp.arange(half_dim, dtype=jnp.float32) * 2.0 / values.shape[-1]))
    angles = positions.astype(jnp.float32)[:, None, None] * frequency
    cosine = jnp.cos(angles)
    sine_part = jnp.sin(angles)
    low_half = values[..., :half_dim]
    high_half = values[..., half_dim:]
    return jnp.concatenate([low_half * cosine - high_half * sine_part, high_half * cosine + low_half * sine_part], -1)

def merge(weight, down_factor, up_factor):
    low_rank = jnp.dot(down_factor, up_factor, preferred_element_type=jnp.float32)
    return (weight.astype(jnp.float32) + SCALE * low_rank).astype(jnp.bfloat16)

def attend_rows(query, cache_keys, cache_values, fresh_keys, fresh_values, lengths):
    groups = HEADS // KV_HEADS
    scaling = 1.0 / math.sqrt(HEAD_DIM)

    def one_row(operands):
        row_query, row_keys, row_values, row_fresh_keys, row_fresh_values, row_length = operands
        grouped = row_query.astype(jnp.float32).reshape(KV_HEADS, groups, HEAD_DIM)
        keys_now = row_keys.astype(jnp.float32)
        values_now = row_values.astype(jnp.float32)
        cache_scores = jnp.einsum('kgd,ckd->kgc', grouped, keys_now) * scaling
        fresh_scores = jnp.einsum('kgd,skd->kgs', grouped, row_fresh_keys.astype(jnp.float32)) * scaling
        in_cache = (jnp.arange(CACHE_SLOTS) < row_length)[None, None, :]
        cache_scores = jnp.where(in_cache, cache_scores, -1e+30)
        highest = jnp.maximum(lax.optimization_barrier(jnp.max(cache_scores, -1)), lax.optimization_barrier(jnp.max(fresh_scores, -1)))[..., None]
        cache_weights = jnp.where(in_cache, jnp.exp(cache_scores - highest), 0.0)
        merged_weights = jnp.exp(fresh_scores - highest)
        denominator = lax.optimization_barrier(jnp.sum(cache_weights, -1, keepdims=True)) + lax.optimization_barrier(jnp.sum(merged_weights, -1, keepdims=True))
        cache_probs = lax.optimization_barrier((cache_weights / denominator).astype(jnp.bfloat16))
        fresh_probs = lax.optimization_barrier((merged_weights / denominator).astype(jnp.bfloat16))
        blended = jnp.einsum('kgc,ckd->kgd', cache_probs.astype(jnp.float32), values_now)
        blended = blended + jnp.einsum('kgs,skd->kgd', fresh_probs.astype(jnp.float32), row_fresh_values.astype(jnp.float32))
        return blended.reshape(QW).astype(jnp.bfloat16)
    return lax.map(one_row, (query, cache_keys, cache_values, fresh_keys, fresh_values, lengths))

def reference(hidden, w_query, w_key, w_value, a_factors, b_query, b_key, b_value, key_cache, value_cache, lengths):
    merged_query = merge(w_query, a_factors[0], b_query)
    merged_key = merge(w_key, a_factors[1], b_key)
    merged_value = merge(w_value, a_factors[2], b_value)
    shaped_keys = key_cache.reshape(ROLLOUT_ROWS, CACHE_SLOTS, KV_HEADS, HEAD_DIM)
    shaped_values = value_cache.reshape(ROLLOUT_ROWS, CACHE_SLOTS, KV_HEADS, HEAD_DIM)
    outputs = []
    key_list = []
    value_list = []
    for step_index in range(STEPS):
        positions = lengths + step_index
        proj_query = jnp.dot(hidden[step_index], merged_query, preferred_element_type=jnp.float32).astype(jnp.bfloat16)
        proj_key = jnp.dot(hidden[step_index], merged_key, preferred_element_type=jnp.float32).astype(jnp.bfloat16)
        proj_value = jnp.dot(hidden[step_index], merged_value, preferred_element_type=jnp.float32).astype(jnp.bfloat16)
        query = rotate(proj_query.astype(jnp.float32).reshape(ROLLOUT_ROWS, HEADS, HEAD_DIM), positions)
        query = query.astype(jnp.bfloat16).reshape(ROLLOUT_ROWS, QW)
        new_key = rotate(proj_key.astype(jnp.float32).reshape(ROLLOUT_ROWS, KV_HEADS, HEAD_DIM), positions).astype(jnp.bfloat16)
        key_list.append(new_key)
        value_list.append(proj_value.reshape(ROLLOUT_ROWS, KV_HEADS, HEAD_DIM))
        outputs.append(attend_rows(query, shaped_keys, shaped_values, jnp.stack(key_list, 1), jnp.stack(value_list, 1), lengths))
    attended = jnp.stack(outputs)
    new_keys = jnp.stack(key_list).reshape(STEPS, ROLLOUT_ROWS, KVW)
    new_values = jnp.stack(value_list).reshape(STEPS, ROLLOUT_ROWS, KVW)
    return (attended, new_keys, new_values)
```

```python
import functools
import math

import jax
import jax.numpy as jnp
from jax import lax
from jax.experimental import pallas as pl
from jax.experimental.pallas import tpu as pltpu
from jax.sharding import PartitionSpec as P

HEAD_DIM = 128
STEPS = 4
THETA = 500000.0
SCALE = 0.5
MESH = pl.DeviceIdType.MESH
F32 = jnp.float32
BF16 = jnp.bfloat16

SLOTS = 1536
KEYS = SLOTS + 128
WIDTH = 8192
HALF = WIDTH // 2


def offset(index):
    return (index * (index + 1) // 2) % 4


def body(
    lengths_ref, hidden_ref, wq_ref, wk_ref, wv_ref, a_ref, bq_ref, bk_ref, bv_ref,
    keys_ref, values_ref, cos_ref, sin_ref,
    out_ref, new_keys_ref, new_values_ref,
    wq, wkv, a_buf, h_buf, k_buf, v_buf,
    b_f32, b_send, b_recv, b_query, b_kv,
    h_f32, h_send, h_recv, g_f32,
    acc_q, acc_kv, q_f32, q_send, q_recv, o_send, o_recv, o_f32,
    local_sem, b_ssem, b_rsem, hx_ssem, hx_rsem, x_ssem, x_rsem, hs_ssem, hs_rsem,
    f_ssem, s_ssem, fwd_ssem, a_rsem, sib_ssem, sib_rsem,
    q_ssem, q_rsem, o_ssem, o_rsem,
):
    r = lax.axis_index("rep")
    t = lax.axis_index("tp")
    y, zl = r // 4, r % 4
    zh, x, c = t // 8, (t // 2) % 4, t % 2
    z = zh * 4 + zl
    other = 1 - c

    def tp_of(high, at_x, core):
        return (high * 4 + at_x) * 2 + core

    def z_step(delta):
        to = (z + 8 + delta) % 8
        return y * 4 + to % 4, tp_of(to // 4, x, c)

    def y_step(delta):
        return ((y + 4 + delta) % 4) * 4 + zl, t

    def pick(first):
        devices = []
        for delta in (1, -1):
            zr, zt = z_step(delta)
            yr, yt = y_step(delta)
            is_y = c if first else other
            devices.append((is_y * yr + (1 - is_y) * zr, is_y * yt + (1 - is_y) * zt))
        return devices

    f_plus, f_minus = pick(True)
    s_plus, s_minus = pick(False)
    sibling = (r, tp_of(zh, x, other))

    def origin(core, slot):
        df, ds = offset(slot // 4), offset(slot % 4)
        at_y = (y + core * df + (1 - core) * ds) % 4
        at_z = (zl + (1 - core) * df + core * ds) % 4
        return at_y * 4 + at_z

    def remote(src, dst, ssem, rsem, device):
        return pltpu.make_async_remote_copy(
            src_ref=src, dst_ref=dst, send_sem=ssem, recv_sem=rsem,
            device_id=device, device_id_type=MESH,
        )

    loads = [
        pltpu.make_async_copy(a_ref.at[:, pl.ds(0, 256)], a_buf.at[r, 0], local_sem.at[0]),
        pltpu.make_async_copy(a_ref.at[:, pl.ds(256, 256)], a_buf.at[r, 1], local_sem.at[1]),
        pltpu.make_async_copy(wq_ref, wq, local_sem.at[2]),
        pltpu.make_async_copy(wk_ref, wkv.at[pl.ds(0, 32)], local_sem.at[3]),
        pltpu.make_async_copy(wv_ref, wkv.at[pl.ds(32, 32)], local_sem.at[4]),
        pltpu.make_async_copy(keys_ref, k_buf.at[pl.ds(0, SLOTS)], local_sem.at[5]),
        pltpu.make_async_copy(values_ref, v_buf.at[pl.ds(0, SLOTS)], local_sem.at[6]),
    ]
    for load in loads:
        load.start()

    barrier = pltpu.get_barrier_semaphore()

    def greet(step, _):
        pl.semaphore_signal(barrier, inc=1, device_id=(r, (t + step) % 16), device_id_type=MESH)
        pl.semaphore_signal(barrier, inc=1, device_id=((r + step) % 16, t), device_id_type=MESH)
        return 0

    lax.fori_loop(1, 16, greet, 0)
    for delta in (1, -1):
        pl.semaphore_signal(barrier, inc=1, device_id=z_step(delta), device_id_type=MESH)

    b_f32[...] = jnp.zeros_like(b_f32)
    up = bq_ref[...].astype(F32)
    up_key = bk_ref[...].astype(F32)
    up_value = bv_ref[...].astype(F32)
    for k in range(4):
        for h in range(4):
            b_f32[8 * k + h : 8 * k + h + 1, :] = up[k : k + 1, 128 * h : 128 * h + 128]
        b_f32[8 * k + 4 : 8 * k + 5, 0:32] = up_key[k : k + 1, :]
        b_f32[8 * k + 5 : 8 * k + 6, 0:32] = up_value[k : k + 1, :]
    b_send[...] = b_f32[0:32, :].astype(BF16)
    own = hidden_ref[...].astype(F32)
    for half in range(2):
        for block in range(4):
            start = half * HALF + block * 1024
            h_f32[half, 4 * block : 4 * block + 4, :] = own[:, start : start + 1024]
    h_send[...] = h_f32[...].astype(BF16)
    k_buf[SLOTS:, :] = jnp.zeros((128, 512), BF16)
    v_buf[SLOTS:, :] = jnp.zeros((128, 512), BF16)
    loads[0].wait()
    loads[1].wait()
    pl.semaphore_wait(barrier, 32)

    def b_copy(step):
        return remote(b_send, b_recv.at[r], b_ssem.at[step], b_rsem.at[step], ((r + step) % 16, t))

    def start_b(step, _):
        b_copy(step).start()
        return 0

    lax.fori_loop(1, 16, start_b, 0)
    b_recv[r] = b_send[...]

    me4 = zh * 2 + c
    hx = []
    for at, (to_high, to_core) in enumerate(((zh, other), (1 - zh, c), (1 - zh, other))):
        hx.append(remote(
            h_send.at[to_core], h_recv.at[me4], hx_ssem.at[at], hx_rsem.at[at],
            (r, tp_of(to_high, x, to_core)),
        ))
    for copy in reversed(hx):
        copy.start()
    h_recv[me4] = h_send[c]

    def f_copy(kind):
        if kind == 0:
            mine = a_buf.at[r, c]
            return remote(mine, mine, f_ssem.at[0], a_rsem.at[8, 0], f_plus)
        if kind == 1:
            mine = a_buf.at[r, c]
            return remote(mine, mine, f_ssem.at[1], a_rsem.at[4, 0], f_minus)
        if kind == 2:
            part = a_buf.at[origin(c, 8), c, pl.ds(0, 96)]
            return remote(part, part, f_ssem.at[2], a_rsem.at[12, 0], f_plus)
        part = a_buf.at[origin(c, 4), c, pl.ds(96, 96)]
        return remote(part, part, f_ssem.at[3], a_rsem.at[12, 1], f_minus)

    def s_copy(index, way):
        chunk = a_buf.at[origin(c, index * 4), c]
        return remote(
            chunk, chunk, s_ssem.at[index, way], a_rsem.at[index * 4 + 2 - way, 0],
            s_plus if way == 0 else s_minus,
        )

    def fwd_copy(index, way):
        part = a_buf.at[origin(c, index * 4 + 2 - way), c, pl.ds(96 * way, 96)]
        return remote(
            part, part, fwd_ssem.at[index, way], a_rsem.at[index * 4 + 3, way],
            s_plus if way == 0 else s_minus,
        )

    def sib_copy(slot):
        chunk = a_buf.at[origin(c, slot), c]
        return remote(chunk, chunk, sib_ssem.at[slot], sib_rsem.at[slot], sibling)

    def sib_in(slot):
        chunk = a_buf.at[origin(other, slot), other]
        return remote(chunk, chunk, sib_ssem.at[slot], sib_rsem.at[slot], sibling)

    def a_in(slot, part=None):
        chunk = a_buf.at[origin(c, slot), c]
        if part is not None:
            chunk = chunk.at[pl.ds(96 * part, 96)]
        return remote(
            chunk, chunk, sib_ssem.at[slot], a_rsem.at[slot, 0 if part is None else part], sibling
        )

    f_copy(0).start()
    f_copy(1).start()
    s_copy(0, 0).start()
    s_copy(0, 1).start()

    def half_of(at_x, core, start=0, size=HALF):
        return h_buf.at[at_x, :, pl.ds(pl.multiple_of(core * HALF + start, 128), size)]

    x_plus = (r, tp_of(zh, (x + 1) % 4, c))
    x_minus = (r, tp_of(zh, (x + 3) % 4, c))

    def x_copy(kind):
        if kind < 2:
            block = half_of(x, c)
            return remote(block, block, x_ssem.at[kind], x_rsem.at[kind], (x_plus, x_minus)[kind])
        source = (x + 3) % 4 if kind == 2 else (x + 1) % 4
        block = half_of(source, c, (kind - 2) * 2048, 2048)
        return remote(block, block, x_ssem.at[kind], x_rsem.at[kind], (x_plus, x_minus)[kind - 2])

    def hs_copy(step):
        block = half_of((x + step) % 4, c)
        return remote(block, block, hs_ssem.at[step], hs_rsem.at[step], sibling)

    def hs_in(step):
        block = half_of((x + step) % 4, other)
        return remote(block, block, hs_ssem.at[step], hs_rsem.at[step], sibling)

    def x_in(kind):
        if kind < 2:
            block = half_of((x + 3) % 4 if kind == 0 else (x + 1) % 4, c)
        else:
            block = half_of((x + 2) % 4, c, (kind - 2) * 2048, 2048)
        return remote(block, block, x_ssem.at[kind], x_rsem.at[kind], sibling)

    for copy in hx:
        copy.wait_recv()
    for k in range(4):
        got = h_recv[k].astype(F32)
        for block in range(4):
            g_f32[4 * k : 4 * k + 4, 1024 * block : 1024 * block + 1024] = got[
                4 * block : 4 * block + 4, :
            ]
    h_buf[x, :, pl.ds(pl.multiple_of(c * HALF, 128), HALF)] = g_f32[...].astype(BF16)
    x_copy(0).start()
    x_copy(1).start()
    hs_copy(0).start()

    def wait_b(step, _):
        b_copy(step).wait_recv()
        return 0

    lax.fori_loop(1, 16, wait_b, 0)
    b_f32[...] = b_recv[...].reshape(512, 128).astype(F32)
    for h in range(4):
        b_query[:, 128 * h : 128 * h + 128] = (SCALE * b_f32[pl.ds(h, 64, stride=8), :]).astype(BF16)
    bk_all = SCALE * b_f32[pl.ds(4, 64, stride=8), :]
    bv_all = SCALE * b_f32[pl.ds(5, 64, stride=8), :]
    b_kv[:, 0:64] = jnp.transpose(bk_all)[0:64, :].astype(BF16)
    b_kv[:, 64:128] = jnp.transpose(pltpu.roll(bv_all, 32, 1))[0:64, :].astype(BF16)

    acc_q[...] = jnp.zeros_like(acc_q)
    acc_kv[...] = jnp.zeros_like(acc_kv)
    for load in loads[2:5]:
        load.wait()

    def merge(at, half):
        start = pl.multiple_of(at * 512 + half * 256, 256)
        down = a_buf[at, half]
        low = lax.dot_general(
            down[0:64], b_query[...], (((0,), (0,)), ((), ())), preferred_element_type=F32
        )
        rows = pl.ds(start, 256)
        wq[rows, :] = (wq[rows, :].astype(F32) + low).astype(BF16)
        low_kv = jnp.dot(b_kv[...], down[64:192], preferred_element_type=F32)
        wkv[:, rows] = (wkv[:, rows].astype(F32) + low_kv).astype(BF16)

    def project(slot):
        start = pl.multiple_of(origin(c, slot) * 512, 512)
        states = h_buf[:, :, pl.ds(start, 512)].reshape(64, 512)
        acc_q[...] += jnp.dot(states, wq[pl.ds(start, 512), :], preferred_element_type=F32)
        acc_kv[...] += lax.dot_general(
            states, wkv[:, pl.ds(start, 512)], (((1,), (1,)), ((), ())), preferred_element_type=F32
        )

    def turn(slot, _):
        index, way = slot // 4, slot % 4

        @pl.when(slot == 1)
        def _():
            a_in(4).wait_recv()
            s_copy(1, 0).start()
            s_copy(1, 1).start()
            f_copy(3).start()
            sib_copy(4).start()

        @pl.when(slot == 2)
        def _():
            a_in(8).wait_recv()
            s_copy(2, 0).start()
            s_copy(2, 1).start()
            f_copy(2).start()
            sib_copy(8).start()

        @pl.when(slot == 3)
        def _():
            a_in(12, 0).wait_recv()
            a_in(12, 1).wait_recv()
            s_copy(3, 0).start()
            s_copy(3, 1).start()
            sib_copy(12).start()

        @pl.when(way == 1)
        def _():
            a_in(slot).wait_recv()
            fwd_copy(index, 1).start()
            sib_copy(slot).start()

        @pl.when(way == 2)
        def _():
            a_in(slot).wait_recv()
            fwd_copy(index, 0).start()
            sib_copy(slot).start()

        @pl.when(way == 3)
        def _():
            a_in(slot, 0).wait_recv()
            a_in(slot, 1).wait_recv()
            sib_copy(slot).start()

        @pl.when(slot == 4)
        def _():
            x_in(0).wait_recv()
            x_in(1).wait_recv()
            x_copy(2).start()
            x_copy(3).start()
            hs_copy(3).start()
            hs_copy(1).start()

        @pl.when(slot == 6)
        def _():
            x_in(2).wait_recv()
            x_in(3).wait_recv()
            hs_copy(2).start()

        @pl.when(slot == 8)
        def _():
            for step in range(4):
                hs_in(step).wait_recv()

        merge(origin(c, slot), c)

        @pl.when(slot > 0)
        def _():
            sib_in(slot).wait_recv()

        merge(origin(other, slot), other)

        return 0

    lax.fori_loop(0, 16, turn, 0)

    def project_turn(slot, _):
        project(slot)
        return 0

    lax.fori_loop(0, 16, project_turn, 0)

    acc = acc_q[...]
    kv = jnp.concatenate([acc_kv[...], jnp.zeros((64, 64), F32)], 1)
    lane = lax.broadcasted_iota(jnp.int32, (64, 128), 1)
    mine = lane // 32 == t % 4
    own_key = jnp.where(mine, pltpu.roll(kv, (t % 4) * 32, 1), 0.0)
    own_value = jnp.where(mine, pltpu.roll(kv, (t % 4) * 32 + 96, 1), 0.0)
    for to in range(16):
        base = ((to // 2) % 4) * 16 + ((to // 8) * 2 + to % 2) * 4
        for h in range(4):
            q_f32[to, 4 * h : 4 * h + 4, :] = acc[base : base + 4, 128 * h : 128 * h + 128]
        q_f32[to, 16:20, :] = own_key[base : base + 4]
        q_f32[to, 20:24, :] = own_value[base : base + 4]
        q_f32[to, 24:32, :] = jnp.zeros((8, 128), F32)
    q_send[...] = q_f32[...].astype(BF16)

    def q_copy(step):
        to = (t + step) % 16
        return remote(q_send.at[to], q_recv.at[t], q_ssem.at[step], q_rsem.at[step], (r, to))

    def start_q(step, _):
        q_copy(step).start()
        return 0

    lax.fori_loop(1, 16, start_q, 0)
    q_recv[t] = q_send[t]
    loads[5].wait()
    loads[6].wait()

    def wait_q(step, _):
        q_copy(step).wait_recv()
        return 0

    lax.fori_loop(1, 16, wait_q, 0)

    cosine, sine = cos_ref[...], sin_ref[...]
    length = lengths_ref[0]
    column = lax.broadcasted_iota(jnp.int32, (64, KEYS), 1)
    step_of = lax.broadcasted_iota(jnp.int32, (64, KEYS), 0) % 4
    valid = (column < length) | ((column >= SLOTS) & (column - SLOTS <= step_of))
    scaling = 1.0 / math.sqrt(HEAD_DIM)

    def rotated(values, cos_rows, sin_rows):
        return values * cos_rows + pltpu.roll(values, 64, values.ndim - 1) * sin_rows

    for g in range(4):
        cols = slice(128 * g, 128 * g + 128)
        fresh = q_recv[4 * g, 16:32, :].astype(F32)
        for u in range(1, 4):
            fresh += q_recv[4 * g + u, 16:32, :].astype(F32)
        fresh_key = rotated(fresh, cosine, sine)[0:4].astype(BF16)
        fresh_value = fresh[4:8].astype(BF16)
        new_keys_ref[:, cols] = fresh_key
        new_values_ref[:, cols] = fresh_value
        pad = jnp.zeros((12, 128), BF16)
        k_buf[SLOTS : SLOTS + 16, cols] = jnp.concatenate([fresh_key, pad], 0)
        v_buf[SLOTS : SLOTS + 16, cols] = jnp.concatenate([fresh_value, pad], 0)
        query = q_recv[4 * g : 4 * g + 4, 0:16, :].astype(F32).reshape(64, 128)
        tables = (jnp.concatenate([cosine] * 4, 0), jnp.concatenate([sine] * 4, 0))
        query = rotated(query, *tables).astype(BF16)
        scores = scaling * lax.dot_general(
            query, k_buf[:, cols], (((1,), (1,)), ((), ())), preferred_element_type=F32
        )
        scores = jnp.where(valid, scores, -1e30)
        highest = jnp.max(scores, -1, keepdims=True)
        weights = jnp.where(valid, jnp.exp(scores - highest), 0.0)
        total = jnp.sum(weights, -1, keepdims=True)
        probs = (weights * (1.0 / total)).astype(BF16)
        blended = jnp.dot(probs, v_buf[:, cols], preferred_element_type=F32).astype(BF16)
        o_send[4 * g : 4 * g + 4] = blended.reshape(4, 16, 128)

    def o_copy(step):
        to = (t + step) % 16
        return remote(o_send.at[to], o_recv.at[t], o_ssem.at[step], o_rsem.at[step], (r, to))

    def start_o(step, _):
        o_copy(step).start()
        return 0

    lax.fori_loop(1, 16, start_o, 0)
    o_recv[t] = o_send[t]

    def wait_o(step, _):
        o_copy(step).wait_recv()
        return 0

    lax.fori_loop(1, 16, wait_o, 0)
    o_f32[...] = o_recv[...].reshape(256, 128).astype(F32)
    for s in range(STEPS):
        for h in range(4):
            out_ref[s, :, 128 * h : 128 * h + 128] = o_f32[
                pl.ds(4 * h + s, 16, stride=16), :
            ].astype(BF16)

    def wait_sends(step, _):
        b_copy(step).wait_send()
        q_copy(step).wait_send()
        o_copy(step).wait_send()
        sib_copy(step).wait_send()
        return 0

    lax.fori_loop(1, 16, wait_sends, 0)
    for copy in hx:
        copy.wait_send()
    for k in range(4):
        f_copy(k).wait_send()
        x_copy(k).wait_send()
        hs_copy(k).wait_send()
        for way in range(2):
            s_copy(k, way).wait_send()
            fwd_copy(k, way).wait_send()


def shards(
    hidden, w_query, w_key, w_value, a_factors, b_query, b_key, b_value,
    key_cache, value_cache, lengths,
):
    half_dim = HEAD_DIM // 2
    frequency = THETA ** (-(jnp.arange(half_dim, dtype=F32) * 2.0 / HEAD_DIM))
    positions = lengths[0] + jnp.arange(16, dtype=jnp.int32) % STEPS
    angles = positions.astype(F32)[:, None] * frequency
    cosine, sine = jnp.cos(angles), jnp.sin(angles)
    cosine = jnp.concatenate([cosine, cosine], 1)
    sine = jnp.concatenate([-sine, sine], 1)

    anywhere = pl.BlockSpec(memory_space=pl.ANY)
    vmem = pl.BlockSpec(memory_space=pltpu.VMEM)
    dma = pltpu.SemaphoreType.DMA
    attended, new_keys, new_values = pl.pallas_call(
        body,
        out_shape=(
            jax.ShapeDtypeStruct((4, 16, 512), BF16),
            jax.ShapeDtypeStruct((4, 512), BF16),
            jax.ShapeDtypeStruct((4, 512), BF16),
        ),
        in_specs=[
            pl.BlockSpec(memory_space=pltpu.SMEM), vmem, anywhere, anywhere, anywhere, anywhere,
            vmem, vmem, vmem, anywhere, anywhere, vmem, vmem,
        ],
        out_specs=(vmem, vmem, vmem),
        scratch_shapes=[
            pltpu.VMEM((WIDTH, 512), BF16),
            pltpu.VMEM((64, WIDTH), BF16),
            pltpu.VMEM((16, 2, 192, 256), BF16),
            pltpu.VMEM((4, 16, WIDTH), BF16),
            pltpu.VMEM((KEYS, 512), BF16),
            pltpu.VMEM((KEYS, 512), BF16),
            pltpu.VMEM((512, 128), F32),
            pltpu.VMEM((32, 128), BF16),
            pltpu.VMEM((16, 32, 128), BF16),
            pltpu.VMEM((64, 512), BF16),
            pltpu.VMEM((64, 128), BF16),
            pltpu.VMEM((2, 16, 1024), F32),
            pltpu.VMEM((2, 16, 1024), BF16),
            pltpu.VMEM((4, 16, 1024), BF16),
            pltpu.VMEM((16, HALF), F32),
            pltpu.VMEM((64, 512), F32),
            pltpu.VMEM((64, 64), F32),
            pltpu.VMEM((16, 32, 128), F32),
            pltpu.VMEM((16, 32, 128), BF16),
            pltpu.VMEM((16, 32, 128), BF16),
            pltpu.VMEM((16, 16, 128), BF16),
            pltpu.VMEM((16, 16, 128), BF16),
            pltpu.VMEM((256, 128), F32),
            dma((7,)), dma((16,)), dma((16,)), dma((3,)), dma((3,)),
            dma((4,)), dma((4,)), dma((4,)), dma((4,)),
            dma((4,)), dma((4, 2)), dma((4, 2)), dma((16, 2)), dma((16,)), dma((16,)),
            dma((16,)), dma((16,)), dma((16,)), dma((16,)),
        ],
        compiler_params=pltpu.CompilerParams(
            collective_id=0, has_side_effects=True, vmem_limit_bytes=48 * 1024 * 1024
        ),
    )(
        lengths, hidden[:, 0], w_query, w_key.T, w_value.T,
        jnp.swapaxes(a_factors, 1, 2).reshape(192, 512), b_query, b_key, b_value,
        key_cache[0], value_cache[0], cosine, sine,
    )
    return attended, new_keys[:, None], new_values[:, None]


def solution(mesh):
    placed = (
        P(None, ("rep", "tp"), None),
        P(None, "tp"),
        P(None, "tp"),
        P(None, "tp"),
        P(None, "rep", None),
        P("rep", "tp"),
        P("rep", "tp"),
        P("rep", "tp"),
        P(("rep", "tp"), None, None),
        P(("rep", "tp"), None, None),
        P(("rep", "tp")),
    )
    return jax.shard_map(
        shards,
        mesh=mesh,
        in_specs=placed,
        out_specs=(
            P(None, "rep", "tp"),
            P(None, ("rep", "tp"), None),
            P(None, ("rep", "tp"), None),
        ),
        check_vma=False,
    )
```

```python
import functools
import math

import jax
import jax.numpy as jnp
from jax import lax
from jax.experimental import pallas as pl
from jax.experimental.pallas import tpu as pltpu
from jax.sharding import PartitionSpec as P

HEAD_DIM = 128
STEPS = 4
THETA = 500000.0
SCALE = 0.5
MESH = pl.DeviceIdType.MESH
F32 = jnp.float32
BF16 = jnp.bfloat16

SLOTS = 1536
LAG, ES, EL, EH = 3, 6, 11, 15
KEYS = SLOTS + 128
WIDTH = 8192
HALF = WIDTH // 2


def offset(index):
    return (index * (index + 1) // 2) % 4


def body(
    lengths_ref, hidden_ref, wq_ref, wk_ref, wv_ref, a_ref, bq_ref, bk_ref, bv_ref,
    keys_ref, values_ref, tables_ref,
    out_ref, new_keys_ref, new_values_ref,
    length_in, hidden_in, bq_in, bk_in, bv_in, wq, wkv, a_buf, h_buf, k_buf, v_buf,
    b_f32, b_send, b_recv, b_query, b_kv,
    h_f32, h_raw, g_f32,
    a_kv, l_f32, l_send, l_recv, p_send, p_recv, t_all, low_f32,
    acc_q, acc_kv, q_f32, q_send, q_recv, o_send, o_recv, o_f32,
    local_sem, b_ssem, b_rsem, z_ssem, h_rsem, x_ssem, hs_ssem, hs_rsem,
    f_ssem, s_ssem, far_ssem, a_rsem, sib_ssem, sib_rsem,
    l_ssem, l_rsem, p_ssem, p_rsem, t_ssem, t_rsem,
    q_ssem, q_rsem, o_ssem, o_rsem,
):
    r = lax.axis_index("rep")
    t = lax.axis_index("tp")
    y, zl = r // 4, r % 4
    zh, x, c = t // 8, (t // 2) % 4, t % 2
    z = zh * 4 + zl
    other = 1 - c

    def tp_of(high, at_x, core):
        return (high * 4 + at_x) * 2 + core

    def z_step(delta):
        to = (z + 8 + delta) % 8
        return y * 4 + to % 4, tp_of(to // 4, x, c)

    def y_step(delta):
        return ((y + 4 + delta) % 4) * 4 + zl, t

    def pick(first):
        devices = []
        for delta in (1, -1, 2, -2):
            zr, zt = z_step(delta)
            yr, yt = y_step(delta)
            is_y = c if first else other
            devices.append((is_y * yr + (1 - is_y) * zr, is_y * yt + (1 - is_y) * zt))
        return devices

    f_plus, f_minus, f_plus2, f_minus2 = pick(True)
    s_plus, s_minus, s_plus2, s_minus2 = pick(False)
    sibling = (r, tp_of(zh, x, other))

    def origin(core, slot):
        df, ds = offset(slot // 4), offset(slot % 4)
        at_y = (y + core * df + (1 - core) * ds) % 4
        at_z = (zl + (1 - core) * df + core * ds) % 4
        return at_y * 4 + at_z

    def remote(src, dst, ssem, rsem, device):
        return pltpu.make_async_remote_copy(
            src_ref=src, dst_ref=dst, send_sem=ssem, recv_sem=rsem,
            device_id=device, device_id_type=MESH,
        )

    small = [
        pltpu.make_async_copy(source, target, local_sem.at[7 + at])
        for at, (source, target) in enumerate((
            (bq_ref, bq_in), (bk_ref, bk_in), (bv_ref, bv_in), (hidden_ref, hidden_in),
            (lengths_ref, length_in),
        ))
    ]
    loads = [
        pltpu.make_async_copy(a_ref.at[pl.ds(0, 64), pl.ds(0, 256)], a_buf.at[r, 0], local_sem.at[0]),
        pltpu.make_async_copy(a_ref.at[pl.ds(0, 64), pl.ds(256, 256)], a_buf.at[r, 1], local_sem.at[1]),
        pltpu.make_async_copy(wq_ref, wq, local_sem.at[2]),
        pltpu.make_async_copy(wk_ref, wkv.at[pl.ds(0, 32)], local_sem.at[3]),
        pltpu.make_async_copy(wv_ref, wkv.at[pl.ds(32, 32)], local_sem.at[4]),
        pltpu.make_async_copy(keys_ref, k_buf.at[pl.ds(0, SLOTS)], local_sem.at[5]),
        pltpu.make_async_copy(values_ref, v_buf.at[pl.ds(0, SLOTS)], local_sem.at[6]),
        pltpu.make_async_copy(a_ref.at[pl.ds(64, 128)], a_kv, local_sem.at[12]),
    ]
    for load in small + loads:
        load.start()

    barrier = pltpu.get_barrier_semaphore()

    def greet(step, _):
        pl.semaphore_signal(barrier, inc=1, device_id=(r, (t + step) % 16), device_id_type=MESH)
        pl.semaphore_signal(barrier, inc=1, device_id=((r + step) % 16, t), device_id_type=MESH)
        return 0

    lax.fori_loop(1, 16, greet, 0)
    for delta in (1, -1, 2, -2):
        pl.semaphore_signal(barrier, inc=1, device_id=z_step(delta), device_id_type=MESH)

    b_f32[...] = jnp.zeros_like(b_f32)
    for load in small[:4]:
        load.wait()
    up = bq_in[...].astype(F32)
    up_key = bk_in[...].astype(F32)
    up_value = bv_in[...].astype(F32)
    for k in range(4):
        for h in range(4):
            b_f32[8 * k + h : 8 * k + h + 1, :] = up[k : k + 1, 128 * h : 128 * h + 128]
        b_f32[8 * k + 4 : 8 * k + 5, 0:32] = up_key[k : k + 1, :]
        b_f32[8 * k + 5 : 8 * k + 6, 0:32] = up_value[k : k + 1, :]
    b_send[...] = b_f32[0:32, :].astype(BF16)
    own = hidden_in[...].astype(F32)
    for half in range(2):
        for block in range(4):
            start = HALF * half + 1024 * block
            h_f32[half, 4 * block : 4 * block + 4, :] = own[:, start : start + 1024]
    h_raw[t] = h_f32[...].astype(BF16)
    for to in range(16):
        for block in range(4):
            start = 512 * to + 128 * block
            l_f32[to, 4 * block : 4 * block + 4, :] = own[:, start : start + 128]
    l_send[...] = l_f32[...].astype(BF16)
    k_buf[SLOTS:, :] = jnp.zeros((128, 512), BF16)
    v_buf[SLOTS:, :] = jnp.zeros((128, 512), BF16)
    loads[0].wait()
    loads[1].wait()
    pl.semaphore_wait(barrier, 34)

    def held(slot, core):
        return h_raw.at[tp_of((zh + slot // 4) % 2, (x + slot) % 4, core)]

    def z_copy(half):
        block = held(0, c).at[half]
        return remote(
            block, block, z_ssem.at[half], h_rsem.at[4 + half, 0], (r, tp_of(1 - zh, x, c))
        )

    def x_copy(part, way):
        block = held(0, c) if part == 0 else held(4, c).at[part - 1]
        return remote(
            block, block, x_ssem.at[part, way], h_rsem.at[3 + part if part else 0, 4 - way],
            (r, tp_of(zh, (x + way) % 4, c)),
        )

    def hs_copy(slot):
        block = held(slot, c)
        return remote(block, block, hs_ssem.at[slot], hs_rsem.at[slot], sibling)

    def h_in(part, way):
        block = held(way, c) if part == 0 else held(4 + way, c).at[part - 1]
        return remote(
            block, block, hs_ssem.at[0], h_rsem.at[3 + part if part else 0, way], sibling
        )

    def hs_in(slot):
        block = held(slot, other)
        return remote(block, block, hs_ssem.at[slot], hs_rsem.at[slot], sibling)

    def arrange(quad):
        for k in range(4):
            for half in range(2):
                got = h_raw[4 * quad + k, half].astype(F32)
                for block in range(4):
                    start = HALF * half + 1024 * block
                    g_f32[4 * k : 4 * k + 4, start : start + 1024] = got[4 * block : 4 * block + 4, :]
        h_buf[quad] = g_f32[...].astype(BF16)

    def b_copy(step):
        return remote(b_send, b_recv.at[r], b_ssem.at[step], b_rsem.at[step], ((r + step) % 16, t))

    def start_b(step, _):
        b_copy(step).start()
        return 0

    def f_copy(kind):
        if kind < 2:
            mine = a_buf.at[r, c]
            return remote(
                mine, mine, f_ssem.at[kind], a_rsem.at[8 - 4 * kind, 0], (f_plus, f_minus)[kind]
            )
        part = a_buf.at[r, c, pl.ds(32 * (kind - 2), 32)]
        return remote(
            part, part, f_ssem.at[kind], a_rsem.at[12, kind - 2], (f_plus2, f_minus2)[kind - 2]
        )

    def s_copy(index, way):
        chunk = a_buf.at[origin(c, index * 4), c]
        return remote(
            chunk, chunk, s_ssem.at[index, way], a_rsem.at[index * 4 + 2 - way, 0],
            s_plus if way == 0 else s_minus,
        )

    def far_copy(index, way):
        part = a_buf.at[origin(c, index * 4), c, pl.ds(32 * way, 32)]
        return remote(
            part, part, far_ssem.at[index, way], a_rsem.at[index * 4 + 3, way],
            s_plus2 if way == 0 else s_minus2,
        )

    def s_start(index):
        s_copy(index, 0).start()
        s_copy(index, 1).start()
        far_copy(index, 0).start()
        far_copy(index, 1).start()

    def sib_copy(slot):
        chunk = a_buf.at[origin(c, slot), c]
        return remote(chunk, chunk, sib_ssem.at[slot], sib_rsem.at[slot], sibling)

    def sib_in(slot):
        chunk = a_buf.at[origin(other, slot), other]
        return remote(chunk, chunk, sib_ssem.at[slot], sib_rsem.at[slot], sibling)

    def a_in(slot, part=None):
        chunk = a_buf.at[origin(c, slot), c]
        if part is not None:
            chunk = chunk.at[pl.ds(32 * part, 32)]
        return remote(
            chunk, chunk, sib_ssem.at[slot], a_rsem.at[slot, 0 if part is None else part], sibling
        )

    def l_copy(step):
        to = (r + step) % 16
        return remote(l_send.at[to], l_recv.at[r], l_ssem.at[step], l_rsem.at[step], (to, t))

    def p_copy(step):
        to = (r + step) % 16
        return remote(p_send.at[to], p_recv.at[r], p_ssem.at[step], p_rsem.at[step], (to, t))

    def t_copy(step):
        to = (t + step) % 16
        return remote(t_all.at[t], t_all.at[t], t_ssem.at[step], t_rsem.at[step], (r, to))

    def t_in(step):
        block = t_all.at[(t + 16 - step) % 16]
        return remote(block, block, t_ssem.at[step], t_rsem.at[step], (r, (t + step) % 16))

    def each(copy, what):
        def one(step, _):
            if what == "start":
                copy(step).start()
            elif what == "wait_recv":
                copy(step).wait_recv()
            else:
                copy(step).wait_send()
            return 0

        lax.fori_loop(1, 16, one, 0)

    each(l_copy, "start")
    z_copy(0).start()
    z_copy(1).start()
    for way in (2, 1, 3):
        x_copy(0, way).start()
    each(b_copy, "start")
    for k in range(4):
        f_copy(k).start()
    hs_copy(0).start()
    s_start(0)
    b_recv[r] = b_send[...]
    l_recv[r] = l_send[r]
    loads[7].wait()

    for index in (1, 2):
        a_in(4 * index).wait_recv()
        s_start(index)
        sib_copy(4 * index).start()
    a_in(12, 0).wait_recv()
    a_in(12, 1).wait_recv()
    s_start(3)
    sib_copy(12).start()
    each(l_copy, "wait_recv")
    slices = l_recv[...].reshape(256, 128)
    block_of = (lax.broadcasted_iota(jnp.int32, (256, 128), 0) // 4) % 4
    sums = jnp.zeros((256, 128), F32)
    for block in range(4):
        sums += lax.dot_general(
            jnp.where(block_of == block, slices, jnp.zeros_like(slices)),
            a_kv[:, 128 * block : 128 * block + 128],
            (((1,), (1,)), ((), ())), preferred_element_type=F32,
        )
    sums = sums.reshape(16, 2, 8, 128)
    p_send[...] = sums[:, 0] + sums[:, 1]
    each(p_copy, "start")
    p_recv[r] = p_send[r]
    for k in (1, 3, 2):
        h_in(0, k).wait_recv()
        hs_copy(k).start()
    h_in(1, 0).wait_recv()
    for to in (2, 1, 3):
        x_copy(1, to).start()

    def wait_b(step, _):
        b_copy(step).wait_recv()
        return 0

    lax.fori_loop(1, 16, wait_b, 0)
    b_f32[...] = b_recv[...].reshape(512, 128).astype(F32)
    for h in range(4):
        b_query[:, 128 * h : 128 * h + 128] = (SCALE * b_f32[pl.ds(h, 64, stride=8), :]).astype(BF16)
    bk_all = SCALE * b_f32[pl.ds(4, 64, stride=8), :]
    bv_all = SCALE * b_f32[pl.ds(5, 64, stride=8), :]
    b_kv[0:64, :] = bk_all.astype(BF16)
    b_kv[64:128, :] = pltpu.roll(bv_all, 32, 1).astype(BF16)

    acc_q[...] = jnp.zeros_like(acc_q)
    acc_kv[...] = jnp.zeros_like(acc_kv)
    for load in loads[2:5]:
        load.wait()

    def merge(at, half):
        start = pl.multiple_of(at * 512 + half * 256, 256)
        down = a_buf[at, half]
        low = lax.dot_general(
            down, b_query[...], (((0,), (0,)), ((), ())), preferred_element_type=F32
        )
        rows = pl.ds(start, 256)
        wq[rows, :] = (wq[rows, :].astype(F32) + low).astype(BF16)

    def project(part):
        start = pl.multiple_of(part * 2048, 2048)
        states = h_buf[:, :, pl.ds(start, 2048)].reshape(64, 2048)
        acc_q[...] += jnp.dot(states, wq[pl.ds(start, 2048), :], preferred_element_type=F32)
        acc_kv[...] += lax.dot_general(
            states, wkv[:, pl.ds(start, 2048)], (((1,), (1,)), ((), ())), preferred_element_type=F32
        )

    def slot_at(at):
        phase, m = at // 4, at % 4
        middle = ((phase + 1) // 2) % 2
        return middle * (8 * (phase - 1) + 4 * (m // 2) + 1 + m % 2) + (1 - middle) * (4 * m + phase)

    def first(at, _):
        merge(origin(c, slot_at(at)), c)
        return 0

    lax.fori_loop(0, LAG, first, 0)
    h_in(2, 0).wait_recv()
    for to in (2, 1, 3):
        x_copy(2, to).start()
    hs_copy(4).start()

    def turn(at, _):
        slot = slot_at(at)

        @pl.when((at > 3) & (at < 12))
        def _():
            a_in(slot).wait_recv()
            sib_copy(slot).start()

        @pl.when(at >= 12)
        def _():
            a_in(slot, 0).wait_recv()
            a_in(slot, 1).wait_recv()
            sib_copy(slot).start()

        @pl.when(at == ES)
        def _():
            for k in range(4):
                hs_in(k).wait_recv()
            for k in range(2):
                arrange(2 * zh + k)

        @pl.when(at == EL)
        def _():
            each(p_copy, "wait_recv")
            total = jnp.sum(p_recv[...], 0)
            t_all[t] = total + pltpu.roll(total, 4, 0)
            each(t_copy, "start")

        @pl.when(at == EH)
        def _():
            for k in (1, 3, 2):
                h_in(1, k).wait_recv()
                h_in(2, k).wait_recv()
                hs_copy(4 + k).start()

        late = slot_at(at - LAG)

        @pl.when(at > LAG)
        def _():
            sib_in(late).wait_recv()

        merge(origin(c, slot), c)
        merge(origin(other, late), other)
        return 0

    lax.fori_loop(LAG, 16, turn, 0)

    def last(at, _):
        sib_in(slot_at(at)).wait_recv()
        merge(origin(other, slot_at(at)), other)
        return 0

    lax.fori_loop(16 - LAG, 16, last, 0)
    for k in range(4, 8):
        hs_in(k).wait_recv()
    for k in range(2):
        arrange(2 * (1 - zh) + k)

    def project_turn(part, _):
        project(part)
        return 0

    lax.fori_loop(0, 4, project_turn, 0)
    each(t_in, "wait_recv")
    low_in = t_all[...].reshape(128, 128)
    low_high = low_in.astype(BF16)
    low_rest = (low_in - low_high.astype(F32)).astype(BF16)
    low = jnp.dot(low_high, b_kv[...], preferred_element_type=F32) + jnp.dot(
        low_rest, b_kv[...], preferred_element_type=F32
    )
    for to in range(16):
        low_f32[4 * to : 4 * to + 4, :] = low[8 * to : 8 * to + 4, :]

    acc = acc_q[...]
    kv = jnp.concatenate([acc_kv[...], jnp.zeros((64, 64), F32)], 1) + low_f32[...]
    lane = lax.broadcasted_iota(jnp.int32, (64, 128), 1)
    mine = lane // 32 == t % 4
    own_key = jnp.where(mine, pltpu.roll(kv, (t % 4) * 32, 1), 0.0)
    own_value = jnp.where(mine, pltpu.roll(kv, (t % 4) * 32 + 96, 1), 0.0)
    for to in range(16):
        base = 4 * to
        for h in range(4):
            q_f32[to, 4 * h : 4 * h + 4, :] = acc[base : base + 4, 128 * h : 128 * h + 128]
        q_f32[to, 16:20, :] = own_key[base : base + 4]
        q_f32[to, 20:24, :] = own_value[base : base + 4]
        q_f32[to, 24:32, :] = jnp.zeros((8, 128), F32)
    q_send[...] = q_f32[...].astype(BF16)

    def q_copy(step):
        to = (t + step) % 16
        return remote(q_send.at[to], q_recv.at[t], q_ssem.at[step], q_rsem.at[step], (r, to))

    def start_q(step, _):
        q_copy(step).start()
        return 0

    lax.fori_loop(1, 16, start_q, 0)
    q_recv[t] = q_send[t]
    loads[5].wait()
    loads[6].wait()

    each(b_copy, "wait_send")
    each(sib_copy, "wait_send")
    each(l_copy, "wait_send")
    each(p_copy, "wait_send")
    each(t_copy, "wait_send")
    for half in range(2):
        z_copy(half).wait_send()
    for slot in range(8):
        hs_copy(slot).wait_send()
    for part in range(3):
        for way in range(1, 4):
            x_copy(part, way).wait_send()
    for k in range(4):
        f_copy(k).wait_send()
        for way in range(2):
            s_copy(k, way).wait_send()
            far_copy(k, way).wait_send()

    def wait_q(step, _):
        q_copy(step).wait_recv()
        return 0

    lax.fori_loop(1, 16, wait_q, 0)

    small[4].wait()
    cosine, sine = tables_ref[0], tables_ref[1]
    length = length_in[0]
    column = lax.broadcasted_iota(jnp.int32, (64, KEYS), 1)
    step_of = lax.broadcasted_iota(jnp.int32, (64, KEYS), 0) % 4
    valid = (column < length) | ((column >= SLOTS) & (column - SLOTS <= step_of))
    scaling = 1.0 / math.sqrt(HEAD_DIM)

    def rotated(values, cos_rows, sin_rows):
        return values * cos_rows + pltpu.roll(values, 64, values.ndim - 1) * sin_rows

    def o_copy(step):
        to = (t + step) % 16
        return remote(o_send.at[to], o_recv.at[t], o_ssem.at[step], o_rsem.at[step], (r, to))

    def start_o(step, _):
        o_copy(step).start()
        return 0

    for g in range(4):
        cols = slice(128 * g, 128 * g + 128)
        fresh = q_recv[4 * g, 16:32, :].astype(F32)
        for u in range(1, 4):
            fresh += q_recv[4 * g + u, 16:32, :].astype(F32)
        fresh_key = rotated(fresh, cosine, sine)[0:4].astype(BF16)
        fresh_value = fresh[4:8].astype(BF16)
        new_keys_ref[:, cols] = fresh_key
        new_values_ref[:, cols] = fresh_value
        pad = jnp.zeros((12, 128), BF16)
        k_buf[SLOTS : SLOTS + 16, cols] = jnp.concatenate([fresh_key, pad], 0)
        v_buf[SLOTS : SLOTS + 16, cols] = jnp.concatenate([fresh_value, pad], 0)
        query = q_recv[4 * g : 4 * g + 4, 0:16, :].astype(F32).reshape(64, 128)
        tables = (jnp.concatenate([cosine] * 4, 0), jnp.concatenate([sine] * 4, 0))
        query = rotated(query, *tables).astype(BF16)
        scores = scaling * lax.dot_general(
            query, k_buf[:, cols], (((1,), (1,)), ((), ())), preferred_element_type=F32
        )
        scores = jnp.where(valid, scores, -1e30)
        highest = jnp.max(scores, -1, keepdims=True)
        weights = jnp.where(valid, jnp.exp(scores - highest), 0.0)
        total = jnp.sum(weights, -1, keepdims=True)
        probs = (weights * (1.0 / total)).astype(BF16)
        blended = jnp.dot(probs, v_buf[:, cols], preferred_element_type=F32).astype(BF16)
        o_send[4 * g : 4 * g + 4] = blended.reshape(4, 16, 128)

    lax.fori_loop(1, 16, start_o, 0)
    o_recv[t] = o_send[t]

    def wait_q_sends(step, _):
        q_copy(step).wait_send()
        return 0

    lax.fori_loop(1, 16, wait_q_sends, 0)

    def wait_o(step, _):
        o_copy(step).wait_recv()
        return 0

    lax.fori_loop(1, 16, wait_o, 0)
    o_f32[...] = o_recv[...].reshape(256, 128).astype(F32)
    for s in range(STEPS):
        for h in range(4):
            out_ref[s, :, 128 * h : 128 * h + 128] = o_f32[
                pl.ds(4 * h + s, 16, stride=16), :
            ].astype(BF16)

    def wait_last(step, _):
        o_copy(step).wait_send()
        return 0

    lax.fori_loop(1, 16, wait_last, 0)


def shards(
    hidden, w_query, w_key, w_value, a_factors, b_query, b_key, b_value,
    key_cache, value_cache, lengths,
):
    half_dim = HEAD_DIM // 2
    frequency = THETA ** (-(jnp.arange(half_dim, dtype=F32) * 2.0 / HEAD_DIM))
    positions = lengths[0] + jnp.arange(16, dtype=jnp.int32) % STEPS
    angles = positions.astype(F32)[:, None] * frequency
    cosine, sine = jnp.cos(angles), jnp.sin(angles)
    tables = jnp.stack(
        [jnp.concatenate([cosine, cosine], 1), jnp.concatenate([-sine, sine], 1)]
    )

    anywhere = pl.BlockSpec(memory_space=pltpu.HBM)
    vmem = pl.BlockSpec(memory_space=pltpu.VMEM)
    dma = pltpu.SemaphoreType.DMA
    attended, new_keys, new_values = pl.pallas_call(
        body,
        out_shape=(
            pltpu.VMEM((4, 16, 512), BF16),
            pltpu.VMEM((4, 512), BF16),
            pltpu.VMEM((4, 512), BF16),
        ),
        in_specs=[anywhere] * 11 + [vmem],
        out_specs=(vmem, vmem, vmem),
        scratch_shapes=[
            pltpu.SMEM((1,), jnp.int32),
            pltpu.VMEM((4, WIDTH), BF16),
            pltpu.VMEM((4, 512), BF16),
            pltpu.VMEM((4, 32), BF16),
            pltpu.VMEM((4, 32), BF16),
            pltpu.VMEM((WIDTH, 512), BF16),
            pltpu.VMEM((64, WIDTH), BF16),
            pltpu.VMEM((16, 2, 64, 256), BF16),
            pltpu.VMEM((4, 16, WIDTH), BF16),
            pltpu.VMEM((KEYS, 512), BF16),
            pltpu.VMEM((KEYS, 512), BF16),
            pltpu.VMEM((512, 128), F32),
            pltpu.VMEM((32, 128), BF16),
            pltpu.VMEM((16, 32, 128), BF16),
            pltpu.VMEM((64, 512), BF16),
            pltpu.VMEM((128, 128), BF16),
            pltpu.VMEM((2, 16, 1024), F32),
            pltpu.VMEM((16, 2, 16, 1024), BF16),
            pltpu.VMEM((16, WIDTH), F32),
            pltpu.VMEM((128, 512), BF16),
            pltpu.VMEM((16, 16, 128), F32),
            pltpu.VMEM((16, 16, 128), BF16),
            pltpu.VMEM((16, 16, 128), BF16),
            pltpu.VMEM((16, 8, 128), F32),
            pltpu.VMEM((16, 8, 128), F32),
            pltpu.VMEM((16, 8, 128), F32),
            pltpu.VMEM((64, 128), F32),
            pltpu.VMEM((64, 512), F32),
            pltpu.VMEM((64, 64), F32),
            pltpu.VMEM((16, 32, 128), F32),
            pltpu.VMEM((16, 32, 128), BF16),
            pltpu.VMEM((16, 32, 128), BF16),
            pltpu.VMEM((16, 16, 128), BF16),
            pltpu.VMEM((16, 16, 128), BF16),
            pltpu.VMEM((256, 128), F32),
            dma((13,)), dma((16,)), dma((16,)), dma((2,)), dma((6, 4)),
            dma((3, 4)), dma((8,)), dma((8,)),
            dma((4,)), dma((4, 2)), dma((4, 2)), dma((16, 2)), dma((16,)), dma((16,)),
            dma((16,)), dma((16,)), dma((16,)), dma((16,)), dma((16,)), dma((16,)),
            dma((16,)), dma((16,)), dma((16,)), dma((16,)),
        ],
        compiler_params=pltpu.CompilerParams(
            collective_id=0, has_side_effects=True, vmem_limit_bytes=62 * 1024 * 1024
        ),
    )(
        lengths, hidden[:, 0], w_query, w_key.T, w_value.T,
        jnp.swapaxes(a_factors, 1, 2).reshape(192, 512), b_query, b_key, b_value,
        key_cache[0], value_cache[0], tables,
    )
    return attended, new_keys[:, None], new_values[:, None]


def solution(mesh):
    placed = (
        P(None, ("rep", "tp"), None),
        P(None, "tp"),
        P(None, "tp"),
        P(None, "tp"),
        P(None, "rep", None),
        P("rep", "tp"),
        P("rep", "tp"),
        P("rep", "tp"),
        P(("rep", "tp"), None, None),
        P(("rep", "tp"), None, None),
        P(("rep", "tp")),
    )
    return jax.shard_map(
        shards,
        mesh=mesh,
        in_specs=placed,
        out_specs=(
            P(None, "rep", "tp"),
            P(None, ("rep", "tp"), None),
            P(None, ("rep", "tp"), None),
        ),
        check_vma=False,
    )
```

```python
import functools
import math

import jax
import jax.numpy as jnp
from jax import lax
from jax.experimental import pallas as pl
from jax.experimental.pallas import tpu as pltpu
from jax.sharding import PartitionSpec as P

HEAD_DIM = 128
STEPS = 4
THETA = 500000.0
SCALE = 0.5
MESH = pl.DeviceIdType.MESH
F32 = jnp.float32
BF16 = jnp.bfloat16

SLOTS = 1536
LAG, ES, EW, EH = 3, 6, 10, 15
KEYS = SLOTS + 128
WIDTH = 8192
HALF = WIDTH // 2


def offset(index):
    return (index * (index + 1) // 2) % 4


def body(
    lengths_ref, hidden_ref, wq_ref, wk_ref, wv_ref, a_ref, bq_ref, bk_ref, bv_ref,
    keys_ref, values_ref,
    out_ref, fresh_ref,
    tables, length_in, hidden_in, bq_in, bk_in, bv_in, wq, wkv, a_buf, h_buf, k_buf, v_buf,
    b_f32, b_send, b_recv, b_query, w_send,
    h_f32, h_raw, g_f32,
    a_kv, l_f32, l_send, l_recv, p_send, p_recv, w_recv, low_f32,
    acc_q, acc_kv, q_f32, q_send, q_recv, n_send, n_recv, o_send, o_recv, o_f32,
    local_sem, b_ssem, b_rsem, z_ssem, h_rsem, x_ssem, hs_ssem, hs_rsem,
    f_ssem, s_ssem, far_ssem, a_rsem, sib_ssem, sib_rsem,
    l_ssem, l_rsem, p_ssem, p_rsem, w_ssem, w_rsem, n_ssem, n_rsem,
    q_ssem, q_rsem, o_ssem, o_rsem,
):
    r = lax.axis_index("rep")
    t = lax.axis_index("tp")
    y, zl = r // 4, r % 4
    zh, x, c = t // 8, (t // 2) % 4, t % 2
    z = zh * 4 + zl
    other = 1 - c

    def tp_of(high, at_x, core):
        return (high * 4 + at_x) * 2 + core

    def z_step(delta):
        to = (z + 8 + delta) % 8
        return y * 4 + to % 4, tp_of(to // 4, x, c)

    def y_step(delta):
        return ((y + 4 + delta) % 4) * 4 + zl, t

    def pick(first):
        devices = []
        for delta in (1, -1, 2, -2):
            zr, zt = z_step(delta)
            yr, yt = y_step(delta)
            is_y = c if first else other
            devices.append((is_y * yr + (1 - is_y) * zr, is_y * yt + (1 - is_y) * zt))
        return devices

    f_plus, f_minus, f_plus2, f_minus2 = pick(True)
    s_plus, s_minus, s_plus2, s_minus2 = pick(False)
    sibling = (r, tp_of(zh, x, other))

    def origin(core, slot):
        df, ds = offset(slot // 4), offset(slot % 4)
        at_y = (y + core * df + (1 - core) * ds) % 4
        at_z = (zl + (1 - core) * df + core * ds) % 4
        return at_y * 4 + at_z

    def remote(src, dst, ssem, rsem, device):
        return pltpu.make_async_remote_copy(
            src_ref=src, dst_ref=dst, send_sem=ssem, recv_sem=rsem,
            device_id=device, device_id_type=MESH,
        )

    small = [
        pltpu.make_async_copy(source, target, local_sem.at[7 + at])
        for at, (source, target) in enumerate((
            (bq_ref, bq_in), (bk_ref, bk_in), (bv_ref, bv_in), (hidden_ref, hidden_in),
            (lengths_ref, length_in),
        ))
    ]
    loads = [
        pltpu.make_async_copy(a_ref.at[pl.ds(0, 64), pl.ds(0, 256)], a_buf.at[r, 0], local_sem.at[0]),
        pltpu.make_async_copy(a_ref.at[pl.ds(0, 64), pl.ds(256, 256)], a_buf.at[r, 1], local_sem.at[1]),
        pltpu.make_async_copy(wq_ref, wq, local_sem.at[2]),
        pltpu.make_async_copy(wk_ref, wkv.at[pl.ds(0, 32)], local_sem.at[3]),
        pltpu.make_async_copy(wv_ref, wkv.at[pl.ds(32, 32)], local_sem.at[4]),
        pltpu.make_async_copy(keys_ref, k_buf.at[pl.ds(0, SLOTS)], local_sem.at[5]),
        pltpu.make_async_copy(values_ref, v_buf.at[pl.ds(0, SLOTS)], local_sem.at[6]),
        pltpu.make_async_copy(a_ref.at[pl.ds(64, 128)], a_kv, local_sem.at[12]),
    ]
    for load in small + loads:
        load.start()

    barrier = pltpu.get_barrier_semaphore()

    def greet(step, _):
        pl.semaphore_signal(barrier, inc=1, device_id=(r, (t + step) % 16), device_id_type=MESH)
        pl.semaphore_signal(barrier, inc=1, device_id=((r + step) % 16, t), device_id_type=MESH)
        return 0

    lax.fori_loop(1, 16, greet, 0)
    for delta in (1, -1, 2, -2):
        pl.semaphore_signal(barrier, inc=1, device_id=z_step(delta), device_id_type=MESH)

    b_f32[...] = jnp.zeros_like(b_f32)
    for load in small[:4]:
        load.wait()
    up = bq_in[...].astype(F32)
    up_key = bk_in[...].astype(F32)
    up_value = bv_in[...].astype(F32)
    for k in range(4):
        for h in range(4):
            b_f32[8 * k + h : 8 * k + h + 1, :] = up[k : k + 1, 128 * h : 128 * h + 128]
        b_f32[8 * k + 4 : 8 * k + 5, 0:32] = up_key[k : k + 1, :]
        b_f32[8 * k + 5 : 8 * k + 6, 0:32] = up_value[k : k + 1, :]
    b_send[...] = b_f32[0:32, :].astype(BF16)
    own = hidden_in[...].astype(F32)
    for half in range(2):
        for block in range(4):
            start = HALF * half + 1024 * block
            h_f32[half, 4 * block : 4 * block + 4, :] = own[:, start : start + 1024]
    h_raw[t] = h_f32[...].astype(BF16)
    for to in range(16):
        for block in range(4):
            start = 512 * to + 128 * block
            l_f32[to, 4 * block : 4 * block + 4, :] = own[:, start : start + 128]
    l_send[...] = l_f32[...].astype(BF16)
    k_buf[SLOTS:, :] = jnp.zeros((128, 512), BF16)
    v_buf[SLOTS:, :] = jnp.zeros((128, 512), BF16)
    small[4].wait()
    lanes = lax.broadcasted_iota(jnp.int32, (16, 128), 1)
    frequency = jnp.exp((lanes % 64).astype(F32) * (-2.0 * math.log(THETA) / HEAD_DIM))
    ahead = lax.broadcasted_iota(jnp.int32, (16, 128), 0) % STEPS
    angles = (length_in[0] + ahead).astype(F32) * frequency
    tables[0] = jnp.cos(angles)
    tables[1] = jnp.where(lanes < 64, -jnp.sin(angles), jnp.sin(angles))
    loads[0].wait()
    loads[1].wait()
    pl.semaphore_wait(barrier, 34)

    def held(slot, core):
        return h_raw.at[tp_of((zh + slot // 4) % 2, (x + slot) % 4, core)]

    def z_copy(half):
        block = held(0, c).at[half]
        return remote(
            block, block, z_ssem.at[half], h_rsem.at[4 + half, 0], (r, tp_of(1 - zh, x, c))
        )

    def x_copy(part, way):
        block = held(0, c) if part == 0 else held(4, c).at[part - 1]
        return remote(
            block, block, x_ssem.at[part, way], h_rsem.at[3 + part if part else 0, 4 - way],
            (r, tp_of(zh, (x + way) % 4, c)),
        )

    def hs_copy(slot):
        block = held(slot, c)
        return remote(block, block, hs_ssem.at[slot], hs_rsem.at[slot], sibling)

    def h_in(part, way):
        block = held(way, c) if part == 0 else held(4 + way, c).at[part - 1]
        return remote(
            block, block, hs_ssem.at[0], h_rsem.at[3 + part if part else 0, way], sibling
        )

    def hs_in(slot):
        block = held(slot, other)
        return remote(block, block, hs_ssem.at[slot], hs_rsem.at[slot], sibling)

    def arrange(quad):
        for k in range(4):
            for half in range(2):
                got = h_raw[4 * quad + k, half].astype(F32)
                for block in range(4):
                    start = HALF * half + 1024 * block
                    g_f32[4 * k : 4 * k + 4, start : start + 1024] = got[4 * block : 4 * block + 4, :]
        h_buf[quad] = g_f32[...].astype(BF16)

    def b_copy(step):
        return remote(b_send, b_recv.at[r], b_ssem.at[step], b_rsem.at[step], ((r + step) % 16, t))

    def start_b(step, _):
        b_copy(step).start()
        return 0

    def f_copy(kind):
        if kind < 2:
            mine = a_buf.at[r, c]
            return remote(
                mine, mine, f_ssem.at[kind], a_rsem.at[8 - 4 * kind, 0], (f_plus, f_minus)[kind]
            )
        part = a_buf.at[r, c, pl.ds(32 * (kind - 2), 32)]
        return remote(
            part, part, f_ssem.at[kind], a_rsem.at[12, kind - 2], (f_plus2, f_minus2)[kind - 2]
        )

    def s_copy(index, way):
        chunk = a_buf.at[origin(c, index * 4), c]
        return remote(
            chunk, chunk, s_ssem.at[index, way], a_rsem.at[index * 4 + 2 - way, 0],
            s_plus if way == 0 else s_minus,
        )

    def far_copy(index, way):
        part = a_buf.at[origin(c, index * 4), c, pl.ds(32 * way, 32)]
        return remote(
            part, part, far_ssem.at[index, way], a_rsem.at[index * 4 + 3, way],
            s_plus2 if way == 0 else s_minus2,
        )

    def s_start(index):
        s_copy(index, 0).start()
        s_copy(index, 1).start()
        far_copy(index, 0).start()
        far_copy(index, 1).start()

    def sib_copy(slot):
        chunk = a_buf.at[origin(c, slot), c]
        return remote(chunk, chunk, sib_ssem.at[slot], sib_rsem.at[slot], sibling)

    def sib_in(slot):
        chunk = a_buf.at[origin(other, slot), other]
        return remote(chunk, chunk, sib_ssem.at[slot], sib_rsem.at[slot], sibling)

    def a_in(slot, part=None):
        chunk = a_buf.at[origin(c, slot), c]
        if part is not None:
            chunk = chunk.at[pl.ds(32 * part, 32)]
        return remote(
            chunk, chunk, sib_ssem.at[slot], a_rsem.at[slot, 0 if part is None else part], sibling
        )

    def l_copy(step):
        to = (r + step) % 16
        return remote(l_send.at[to], l_recv.at[r], l_ssem.at[step], l_rsem.at[step], (to, t))

    def p_copy(step):
        to = (r + step) % 16
        return remote(p_send.at[to], p_recv.at[r], p_ssem.at[step], p_rsem.at[step], (to, t))

    def w_copy(step):
        to = (t + step) % 16
        return remote(w_send, w_recv.at[t], w_ssem.at[step], w_rsem.at[step], (r, to))

    def each(copy, what):
        def one(step, _):
            if what == "start":
                copy(step).start()
            elif what == "wait_recv":
                copy(step).wait_recv()
            else:
                copy(step).wait_send()
            return 0

        lax.fori_loop(1, 16, one, 0)

    z_copy(0).start()
    z_copy(1).start()
    for k in range(4):
        f_copy(k).start()
    each(b_copy, "start")
    for way in (2, 1, 3):
        x_copy(0, way).start()
    each(l_copy, "start")
    hs_copy(0).start()
    s_start(0)
    b_recv[r] = b_send[...]
    l_recv[r] = l_send[r]
    loads[7].wait()

    for index in (1, 2):
        a_in(4 * index).wait_recv()
        s_start(index)
        sib_copy(4 * index).start()
    a_in(12, 0).wait_recv()
    a_in(12, 1).wait_recv()
    s_start(3)
    sib_copy(12).start()
    for k in (1, 3, 2):
        h_in(0, k).wait_recv()
        hs_copy(k).start()
    h_in(1, 0).wait_recv()
    for to in (2, 1, 3):
        x_copy(1, to).start()

    def wait_b(step, _):
        b_copy(step).wait_recv()
        return 0

    lax.fori_loop(1, 16, wait_b, 0)
    b_f32[...] = b_recv[...].reshape(512, 128).astype(F32)
    for h in range(4):
        b_query[:, 128 * h : 128 * h + 128] = (SCALE * b_f32[pl.ds(h, 64, stride=8), :]).astype(BF16)
    bk_all = SCALE * b_f32[pl.ds(4, 64, stride=8), :]
    bv_all = SCALE * b_f32[pl.ds(5, 64, stride=8), :]
    both = bk_all + pltpu.roll(bv_all, 32, 1)
    w_send[...] = (both[0:32] + pltpu.roll(both[32:64], 64, 1)).astype(BF16)
    w_recv[t] = w_send[...]

    acc_q[...] = jnp.zeros_like(acc_q)
    acc_kv[...] = jnp.zeros_like(acc_kv)
    for load in loads[2:5]:
        load.wait()

    def merge(at, half):
        start = pl.multiple_of(at * 512 + half * 256, 256)
        down = a_buf[at, half]
        low = lax.dot_general(
            down, b_query[...], (((0,), (0,)), ((), ())), preferred_element_type=F32
        )
        rows = pl.ds(start, 256)
        wq[rows, :] = (wq[rows, :].astype(F32) + low).astype(BF16)

    def project(part):
        start = pl.multiple_of(part * 2048, 2048)
        states = h_buf[:, :, pl.ds(start, 2048)].reshape(64, 2048)
        acc_q[...] += jnp.dot(states, wq[pl.ds(start, 2048), :], preferred_element_type=F32)
        acc_kv[...] += lax.dot_general(
            states, wkv[:, pl.ds(start, 2048)], (((1,), (1,)), ((), ())), preferred_element_type=F32
        )

    def slot_at(at):
        phase, m = at // 4, at % 4
        middle = ((phase + 1) // 2) % 2
        return middle * (8 * (phase - 1) + 4 * (m // 2) + 1 + m % 2) + (1 - middle) * (4 * m + phase)

    def first(at, _):
        merge(origin(c, slot_at(at)), c)
        return 0

    lax.fori_loop(0, LAG, first, 0)
    h_in(2, 0).wait_recv()
    for to in (2, 1, 3):
        x_copy(2, to).start()
    hs_copy(4).start()

    each(l_copy, "wait_recv")
    slices = l_recv[...].reshape(256, 128)
    block_of = (lax.broadcasted_iota(jnp.int32, (256, 128), 0) // 4) % 4
    sums = jnp.zeros((256, 128), F32)
    for block in range(4):
        sums += lax.dot_general(
            jnp.where(block_of == block, slices, jnp.zeros_like(slices)),
            a_kv[:, 128 * block : 128 * block + 128],
            (((1,), (1,)), ((), ())), preferred_element_type=F32,
        )
    sums = sums.reshape(16, 2, 8, 128)
    p_send[...] = sums[:, 0] + sums[:, 1]
    each(p_copy, "start")
    p_recv[r] = p_send[r]

    def turn(at, _):
        slot = slot_at(at)

        @pl.when((at > 3) & (at < 12))
        def _():
            a_in(slot).wait_recv()
            sib_copy(slot).start()

        @pl.when(at >= 12)
        def _():
            a_in(slot, 0).wait_recv()
            a_in(slot, 1).wait_recv()
            sib_copy(slot).start()

        @pl.when(at == ES)
        def _():
            for k in range(4):
                hs_in(k).wait_recv()
            for k in range(2):
                arrange(2 * zh + k)

        @pl.when(at == EW)
        def _():
            each(w_copy, "start")

        @pl.when(at == EH)
        def _():
            for k in (1, 3, 2):
                h_in(1, k).wait_recv()
                h_in(2, k).wait_recv()
                hs_copy(4 + k).start()

        late = slot_at(at - LAG)

        @pl.when(at > LAG)
        def _():
            sib_in(late).wait_recv()

        merge(origin(c, slot), c)
        merge(origin(other, late), other)
        return 0

    lax.fori_loop(LAG, 16, turn, 0)

    def last(at, _):
        sib_in(slot_at(at)).wait_recv()
        merge(origin(other, slot_at(at)), other)
        return 0

    lax.fori_loop(16 - LAG, 16, last, 0)
    for k in range(4, 8):
        hs_in(k).wait_recv()
    for k in range(2):
        arrange(2 * (1 - zh) + k)

    def project_turn(part, _):
        project(part)
        return 0

    lax.fori_loop(0, 4, project_turn, 0)
    acc = acc_q[...]
    kv = jnp.concatenate([acc_kv[...], jnp.zeros((64, 64), F32)], 1)
    lane = lax.broadcasted_iota(jnp.int32, (64, 128), 1)
    mine = lane // 32 == t % 4
    own_key = jnp.where(mine, pltpu.roll(kv, (t % 4) * 32, 1), 0.0)
    own_value = jnp.where(mine, pltpu.roll(kv, (t % 4) * 32 + 96, 1), 0.0)
    for to in range(16):
        base = 4 * to
        for h in range(4):
            q_f32[to, 4 * h : 4 * h + 4, :] = acc[base : base + 4, 128 * h : 128 * h + 128]
        n_send[to, 0:4, :] = own_key[base : base + 4]
        n_send[to, 4:8, :] = own_value[base : base + 4]
    q_send[...] = q_f32[...].astype(BF16)

    def q_copy(step):
        to = (t + step) % 16
        return remote(q_send.at[to], q_recv.at[t], q_ssem.at[step], q_rsem.at[step], (r, to))

    def n_copy(step):
        to = (t + step) % 16
        return remote(n_send.at[to], n_recv.at[t], n_ssem.at[step], n_rsem.at[step], (r, to))

    def start_q(step, _):
        q_copy(step).start()
        n_copy(step).start()
        return 0

    lax.fori_loop(1, 16, start_q, 0)
    q_recv[t] = q_send[t]
    n_recv[t] = n_send[t]
    loads[5].wait()
    loads[6].wait()

    each(b_copy, "wait_send")
    each(sib_copy, "wait_send")
    each(l_copy, "wait_send")
    each(p_copy, "wait_send")
    each(w_copy, "wait_send")
    for half in range(2):
        z_copy(half).wait_send()
    for slot in range(8):
        hs_copy(slot).wait_send()
    for part in range(3):
        for way in range(1, 4):
            x_copy(part, way).wait_send()
    for k in range(4):
        f_copy(k).wait_send()
        for way in range(2):
            s_copy(k, way).wait_send()
            far_copy(k, way).wait_send()

    each(p_copy, "wait_recv")
    each(w_copy, "wait_recv")
    total = jnp.sum(p_recv[...], 0)
    total = total + pltpu.roll(total, 4, 0)
    total_high = total.astype(BF16).astype(F32)
    total_rest = total - total_high
    key_rank = lax.broadcasted_iota(jnp.int32, (8, 128), 1) < 64
    totals = jnp.concatenate(
        [
            jnp.where(key_rank, total_high, 0.0),
            jnp.where(key_rank, total_rest, 0.0),
            jnp.where(key_rank, 0.0, total_high),
            jnp.where(key_rank, 0.0, total_rest),
        ],
        0,
    ).astype(BF16)
    key_row = lax.broadcasted_iota(jnp.int32, (8, 128), 0) < 4
    quarter = lax.broadcasted_iota(jnp.int32, (32, 128), 1) // 32
    for g in range(4):
        ups = [jnp.zeros((32, 128), F32) for _ in range(4)]
        for u in range(4):
            block = w_recv[4 * g + u].astype(F32)
            for at, held_at in enumerate((0, 2, 1, 3)):
                shift = (32 * u - 32 * held_at) % 128
                moved = pltpu.roll(block, shift, 1) if shift else block
                ups[at] += jnp.where(quarter == u, moved, 0.0)
        up_all = jnp.concatenate(ups, 0).astype(BF16)
        low = jnp.dot(totals, up_all, preferred_element_type=F32)
        low_f32[g] = jnp.where(key_row, low[0:8] + low[8:16], low[16:24] + low[24:32])

    def wait_q(step, _):
        q_copy(step).wait_recv()
        n_copy(step).wait_recv()
        return 0

    lax.fori_loop(1, 16, wait_q, 0)

    cosine, sine = tables[0], tables[1]
    length = length_in[0]
    column = lax.broadcasted_iota(jnp.int32, (64, KEYS), 1)
    step_of = lax.broadcasted_iota(jnp.int32, (64, KEYS), 0) % 4
    valid = (column < length) | ((column >= SLOTS) & (column - SLOTS <= step_of))
    scaling = 1.0 / math.sqrt(HEAD_DIM)

    def rotated(values, cos_rows, sin_rows):
        return values * cos_rows + pltpu.roll(values, 64, values.ndim - 1) * sin_rows

    def o_copy(step):
        to = (t + step) % 16
        return remote(o_send.at[to], o_recv.at[t], o_ssem.at[step], o_rsem.at[step], (r, to))

    def start_o(step, _):
        o_copy(step).start()
        return 0

    for g in range(4):
        cols = slice(128 * g, 128 * g + 128)
        fresh = n_recv[4 * g] + n_recv[4 * g + 1] + n_recv[4 * g + 2] + n_recv[4 * g + 3]
        fresh = (fresh + low_f32[g]).astype(BF16)
        fresh_key = rotated(fresh.astype(F32), cosine[0:8], sine[0:8])[0:4].astype(BF16)
        fresh_value = fresh[4:8]
        fresh_ref[0, :, cols] = fresh_key
        fresh_ref[1, :, cols] = fresh_value
        pad = jnp.zeros((12, 128), BF16)
        k_buf[SLOTS : SLOTS + 16, cols] = jnp.concatenate([fresh_key, pad], 0)
        v_buf[SLOTS : SLOTS + 16, cols] = jnp.concatenate([fresh_value, pad], 0)
        query = q_recv[4 * g : 4 * g + 4].astype(F32).reshape(64, 128)
        tables = (jnp.concatenate([cosine] * 4, 0), jnp.concatenate([sine] * 4, 0))
        query = rotated(query, *tables).astype(BF16)
        scores = scaling * lax.dot_general(
            query, k_buf[:, cols], (((1,), (1,)), ((), ())), preferred_element_type=F32
        )
        scores = jnp.where(valid, scores, -1e30)
        highest = jnp.max(scores, -1, keepdims=True)
        weights = jnp.where(valid, jnp.exp(scores - highest), 0.0)
        total = jnp.sum(weights, -1, keepdims=True)
        probs = (weights * (1.0 / total)).astype(BF16)
        blended = jnp.dot(probs, v_buf[:, cols], preferred_element_type=F32).astype(BF16)
        o_send[4 * g : 4 * g + 4] = blended.reshape(4, 16, 128)

    lax.fori_loop(1, 16, start_o, 0)
    o_recv[t] = o_send[t]

    def wait_q_sends(step, _):
        q_copy(step).wait_send()
        n_copy(step).wait_send()
        return 0

    lax.fori_loop(1, 16, wait_q_sends, 0)

    def wait_o(step, _):
        o_copy(step).wait_recv()
        return 0

    lax.fori_loop(1, 16, wait_o, 0)
    o_f32[...] = o_recv[...].reshape(256, 128).astype(F32)
    for s in range(STEPS):
        for h in range(4):
            out_ref[s, :, 128 * h : 128 * h + 128] = o_f32[
                pl.ds(4 * h + s, 16, stride=16), :
            ].astype(BF16)

    def wait_last(step, _):
        o_copy(step).wait_send()
        return 0

    lax.fori_loop(1, 16, wait_last, 0)


def shards(
    hidden, w_query, w_key, w_value, a_factors, b_query, b_key, b_value,
    key_cache, value_cache, lengths,
):
    anywhere = pl.BlockSpec(memory_space=pltpu.HBM)
    vmem = pl.BlockSpec(memory_space=pltpu.VMEM)
    dma = pltpu.SemaphoreType.DMA
    attended, fresh = pl.pallas_call(
        body,
        out_shape=(
            pltpu.VMEM((4, 16, 512), BF16),
            pltpu.VMEM((2, 4, 512), BF16),
        ),
        in_specs=[anywhere] * 11,
        out_specs=(vmem, vmem),
        scratch_shapes=[
            pltpu.VMEM((2, 16, 128), F32),
            pltpu.SMEM((1,), jnp.int32),
            pltpu.VMEM((4, WIDTH), BF16),
            pltpu.VMEM((4, 512), BF16),
            pltpu.VMEM((4, 32), BF16),
            pltpu.VMEM((4, 32), BF16),
            pltpu.VMEM((WIDTH, 512), BF16),
            pltpu.VMEM((64, WIDTH), BF16),
            pltpu.VMEM((16, 2, 64, 256), BF16),
            pltpu.VMEM((4, 16, WIDTH), BF16),
            pltpu.VMEM((KEYS, 512), BF16),
            pltpu.VMEM((KEYS, 512), BF16),
            pltpu.VMEM((512, 128), F32),
            pltpu.VMEM((32, 128), BF16),
            pltpu.VMEM((16, 32, 128), BF16),
            pltpu.VMEM((64, 512), BF16),
            pltpu.VMEM((32, 128), BF16),
            pltpu.VMEM((2, 16, 1024), F32),
            pltpu.VMEM((16, 2, 16, 1024), BF16),
            pltpu.VMEM((16, WIDTH), F32),
            pltpu.VMEM((128, 512), BF16),
            pltpu.VMEM((16, 16, 128), F32),
            pltpu.VMEM((16, 16, 128), BF16),
            pltpu.VMEM((16, 16, 128), BF16),
            pltpu.VMEM((16, 8, 128), F32),
            pltpu.VMEM((16, 8, 128), F32),
            pltpu.VMEM((16, 32, 128), BF16),
            pltpu.VMEM((4, 8, 128), F32),
            pltpu.VMEM((64, 512), F32),
            pltpu.VMEM((64, 64), F32),
            pltpu.VMEM((16, 16, 128), F32),
            pltpu.VMEM((16, 16, 128), BF16),
            pltpu.VMEM((16, 16, 128), BF16),
            pltpu.VMEM((16, 8, 128), F32),
            pltpu.VMEM((16, 8, 128), F32),
            pltpu.VMEM((16, 16, 128), BF16),
            pltpu.VMEM((16, 16, 128), BF16),
            pltpu.VMEM((256, 128), F32),
            dma((13,)), dma((16,)), dma((16,)), dma((2,)), dma((6, 4)),
            dma((3, 4)), dma((8,)), dma((8,)),
            dma((4,)), dma((4, 2)), dma((4, 2)), dma((16, 2)), dma((16,)), dma((16,)),
            dma((16,)), dma((16,)), dma((16,)), dma((16,)), dma((16,)), dma((16,)),
            dma((16,)), dma((16,)),
            dma((16,)), dma((16,)), dma((16,)), dma((16,)),
        ],
        compiler_params=pltpu.CompilerParams(
            collective_id=0, has_side_effects=True, vmem_limit_bytes=62 * 1024 * 1024
        ),
    )(
        lengths, hidden[:, 0], w_query, w_key.T, w_value.T,
        jnp.swapaxes(a_factors, 1, 2).reshape(192, 512), b_query, b_key, b_value,
        key_cache[0], value_cache[0],
    )
    return attended, fresh[0][:, None], fresh[1][:, None]


def solution(mesh):
    placed = (
        P(None, ("rep", "tp"), None),
        P(None, "tp"),
        P(None, "tp"),
        P(None, "tp"),
        P(None, "rep", None),
        P("rep", "tp"),
        P("rep", "tp"),
        P("rep", "tp"),
        P(("rep", "tp"), None, None),
        P(("rep", "tp"), None, None),
        P(("rep", "tp")),
    )
    return jax.shard_map(
        shards,
        mesh=mesh,
        in_specs=placed,
        out_specs=(
            P(None, "rep", "tp"),
            P(None, ("rep", "tp"), None),
            P(None, ("rep", "tp"), None),
        ),
        check_vma=False,
    )
```

```python
import functools
import math

import jax
import jax.numpy as jnp
from jax import lax
from jax.experimental import pallas as pl
from jax.experimental.pallas import tpu as pltpu
from jax.sharding import PartitionSpec as P

HEAD_DIM = 128
STEPS = 4
THETA = 500000.0
SCALE = 0.5
MESH = pl.DeviceIdType.MESH
F32 = jnp.float32
BF16 = jnp.bfloat16

SLOTS = 1536
LAG, ES, EW, EH = 4, 8, 12, 15
KEYS = SLOTS + 128
WIDTH = 8192
HALF = WIDTH // 2


def offset(index):
    return (index * (index + 1) // 2) % 4


def body(
    lengths_ref, hidden_ref, wq_ref, wk_ref, wv_ref, a_ref, bq_ref, bk_ref, bv_ref,
    keys_ref, values_ref,
    out_ref, fresh_ref,
    tables, length_in, hidden_in, bq_in, bk_in, bv_in, wq, wkv, a_buf, h_buf, k_buf, v_buf,
    b_f32, b_send, b_recv, b_query, w_send,
    h_f32, h_raw, g_f32,
    a_kv, l_f32, l_send, l_recv, p_send, p_recv, w_recv, low_f32,
    acc_q, acc_kv, q_f32, q_send, q_recv, n_send, n_recv, o_send, o_recv, o_f32,
    local_sem, b_ssem, b_rsem, z_ssem, h_rsem, x_ssem, hs_ssem, hs_rsem,
    f_ssem, s_ssem, far_ssem, a_rsem, sib_ssem, sib_rsem,
    l_ssem, l_rsem, p_ssem, p_rsem, w_ssem, w_rsem, n_ssem, n_rsem,
    q_ssem, q_rsem, o_ssem, o_rsem,
):
    r = lax.axis_index("rep")
    t = lax.axis_index("tp")
    y, zl = r // 4, r % 4
    zh, x, c = t // 8, (t // 2) % 4, t % 2
    z = zh * 4 + zl
    other = 1 - c

    def tp_of(high, at_x, core):
        return (high * 4 + at_x) * 2 + core

    def z_step(delta):
        to = (z + 8 + delta) % 8
        return y * 4 + to % 4, tp_of(to // 4, x, c)

    def y_step(delta):
        return ((y + 4 + delta) % 4) * 4 + zl, t

    def pick(first):
        devices = []
        for delta in (1, -1, 2, -2):
            zr, zt = z_step(delta)
            yr, yt = y_step(delta)
            is_y = c if first else other
            devices.append((is_y * yr + (1 - is_y) * zr, is_y * yt + (1 - is_y) * zt))
        return devices

    f_plus, f_minus, f_plus2, f_minus2 = pick(True)
    s_plus, s_minus, s_plus2, s_minus2 = pick(False)
    sibling = (r, tp_of(zh, x, other))

    def origin(core, slot):
        df, ds = offset(slot // 4), offset(slot % 4)
        at_y = (y + core * df + (1 - core) * ds) % 4
        at_z = (zl + (1 - core) * df + core * ds) % 4
        return at_y * 4 + at_z

    def remote(src, dst, ssem, rsem, device):
        return pltpu.make_async_remote_copy(
            src_ref=src, dst_ref=dst, send_sem=ssem, recv_sem=rsem,
            device_id=device, device_id_type=MESH,
        )

    small = [
        pltpu.make_async_copy(source, target, local_sem.at[7 + at])
        for at, (source, target) in enumerate((
            (bq_ref, bq_in), (bk_ref, bk_in), (bv_ref, bv_in), (hidden_ref, hidden_in),
            (lengths_ref, length_in),
        ))
    ]
    loads = [
        pltpu.make_async_copy(a_ref.at[pl.ds(0, 64), pl.ds(0, 256)], a_buf.at[r, 0], local_sem.at[0]),
        pltpu.make_async_copy(a_ref.at[pl.ds(0, 64), pl.ds(256, 256)], a_buf.at[r, 1], local_sem.at[1]),
        pltpu.make_async_copy(wq_ref, wq, local_sem.at[2]),
        pltpu.make_async_copy(wk_ref, wkv.at[pl.ds(0, 32)], local_sem.at[3]),
        pltpu.make_async_copy(wv_ref, wkv.at[pl.ds(32, 32)], local_sem.at[4]),
        pltpu.make_async_copy(keys_ref, k_buf.at[pl.ds(0, SLOTS)], local_sem.at[5]),
        pltpu.make_async_copy(values_ref, v_buf.at[pl.ds(0, SLOTS)], local_sem.at[6]),
        pltpu.make_async_copy(a_ref.at[pl.ds(64, 128)], a_kv, local_sem.at[12]),
    ]
    for load in small + loads:
        load.start()

    barrier = pltpu.get_barrier_semaphore()

    def greet(step, _):
        pl.semaphore_signal(barrier, inc=1, device_id=(r, (t + step) % 16), device_id_type=MESH)
        pl.semaphore_signal(barrier, inc=1, device_id=((r + step) % 16, t), device_id_type=MESH)
        return 0

    lax.fori_loop(1, 16, greet, 0)
    for delta in (1, -1, 2, -2):
        pl.semaphore_signal(barrier, inc=1, device_id=z_step(delta), device_id_type=MESH)

    b_f32[...] = jnp.zeros_like(b_f32)
    for load in small[:4]:
        load.wait()
    up = bq_in[...].astype(F32)
    up_key = bk_in[...].astype(F32)
    up_value = bv_in[...].astype(F32)
    for k in range(4):
        for h in range(4):
            b_f32[8 * k + h : 8 * k + h + 1, :] = up[k : k + 1, 128 * h : 128 * h + 128]
        b_f32[8 * k + 4 : 8 * k + 5, 0:32] = up_key[k : k + 1, :]
        b_f32[8 * k + 5 : 8 * k + 6, 0:32] = up_value[k : k + 1, :]
    b_send[...] = b_f32[0:32, :].astype(BF16)
    own = hidden_in[...].astype(F32)
    for half in range(2):
        for block in range(4):
            start = HALF * half + 1024 * block
            h_f32[half, 4 * block : 4 * block + 4, :] = own[:, start : start + 1024]
    h_raw[t] = h_f32[...].astype(BF16)
    for to in range(16):
        for block in range(4):
            start = 512 * to + 128 * block
            l_f32[to, 4 * block : 4 * block + 4, :] = own[:, start : start + 128]
    l_send[...] = l_f32[...].astype(BF16)
    k_buf[SLOTS:, :] = jnp.zeros((128, 512), BF16)
    v_buf[SLOTS:, :] = jnp.zeros((128, 512), BF16)
    small[4].wait()
    lanes = lax.broadcasted_iota(jnp.int32, (16, 128), 1)
    frequency = jnp.exp((lanes % 64).astype(F32) * (-2.0 * math.log(THETA) / HEAD_DIM))
    ahead = lax.broadcasted_iota(jnp.int32, (16, 128), 0) % STEPS
    angles = (length_in[0] + ahead).astype(F32) * frequency
    tables[0] = jnp.cos(angles)
    tables[1] = jnp.where(lanes < 64, -jnp.sin(angles), jnp.sin(angles))
    loads[0].wait()
    loads[1].wait()
    pl.semaphore_wait(barrier, 34)

    def held(slot, core):
        return h_raw.at[tp_of((zh + slot // 4) % 2, (x + slot) % 4, core)]

    def z_copy(half):
        block = held(0, c).at[half]
        return remote(
            block, block, z_ssem.at[half], h_rsem.at[4 + half, 0], (r, tp_of(1 - zh, x, c))
        )

    def x_copy(part, way):
        block = held(0, c) if part == 0 else held(4, c).at[part - 1]
        return remote(
            block, block, x_ssem.at[part, way], h_rsem.at[3 + part if part else 0, 4 - way],
            (r, tp_of(zh, (x + way) % 4, c)),
        )

    def hs_copy(slot):
        block = held(slot, c)
        return remote(block, block, hs_ssem.at[slot], hs_rsem.at[slot], sibling)

    def h_in(part, way):
        block = held(way, c) if part == 0 else held(4 + way, c).at[part - 1]
        return remote(
            block, block, hs_ssem.at[0], h_rsem.at[3 + part if part else 0, way], sibling
        )

    def hs_in(slot):
        block = held(slot, other)
        return remote(block, block, hs_ssem.at[slot], hs_rsem.at[slot], sibling)

    def arrange(quad):
        for k in range(4):
            for half in range(2):
                got = h_raw[4 * quad + k, half].astype(F32)
                for block in range(4):
                    start = HALF * half + 1024 * block
                    g_f32[4 * k : 4 * k + 4, start : start + 1024] = got[4 * block : 4 * block + 4, :]
        h_buf[quad] = g_f32[...].astype(BF16)

    def b_copy(step):
        return remote(b_send, b_recv.at[r], b_ssem.at[step], b_rsem.at[step], ((r + step) % 16, t))

    def start_b(step, _):
        b_copy(step).start()
        return 0

    def f_copy(kind):
        if kind < 2:
            mine = a_buf.at[r, c]
            return remote(
                mine, mine, f_ssem.at[kind], a_rsem.at[8 - 4 * kind, 0], (f_plus, f_minus)[kind]
            )
        part = a_buf.at[r, c, pl.ds(32 * (kind - 2), 32)]
        return remote(
            part, part, f_ssem.at[kind], a_rsem.at[12, kind - 2], (f_plus2, f_minus2)[kind - 2]
        )

    def s_copy(index, way):
        chunk = a_buf.at[origin(c, index * 4), c]
        return remote(
            chunk, chunk, s_ssem.at[index, way], a_rsem.at[index * 4 + 2 - way, 0],
            s_plus if way == 0 else s_minus,
        )

    def far_copy(index, way):
        part = a_buf.at[origin(c, index * 4), c, pl.ds(32 * way, 32)]
        return remote(
            part, part, far_ssem.at[index, way], a_rsem.at[index * 4 + 3, way],
            s_plus2 if way == 0 else s_minus2,
        )

    def s_start(index):
        s_copy(index, 0).start()
        s_copy(index, 1).start()
        far_copy(index, 0).start()
        far_copy(index, 1).start()

    def sib_copy(slot):
        chunk = a_buf.at[origin(c, slot), c]
        return remote(chunk, chunk, sib_ssem.at[slot], sib_rsem.at[slot], sibling)

    def sib_in(slot):
        chunk = a_buf.at[origin(other, slot), other]
        return remote(chunk, chunk, sib_ssem.at[slot], sib_rsem.at[slot], sibling)

    def a_in(slot, part=None):
        chunk = a_buf.at[origin(c, slot), c]
        if part is not None:
            chunk = chunk.at[pl.ds(32 * part, 32)]
        return remote(
            chunk, chunk, sib_ssem.at[slot], a_rsem.at[slot, 0 if part is None else part], sibling
        )

    def l_copy(step):
        to = (r + step) % 16
        return remote(l_send.at[to], l_recv.at[r], l_ssem.at[step], l_rsem.at[step], (to, t))

    def p_copy(step):
        to = (r + step) % 16
        return remote(p_send.at[to], p_recv.at[r], p_ssem.at[step], p_rsem.at[step], (to, t))

    def w_copy(step):
        to = (t + step) % 16
        return remote(w_send, w_recv.at[t], w_ssem.at[step], w_rsem.at[step], (r, to))

    def each(copy, what):
        def one(step, _):
            if what == "start":
                copy(step).start()
            elif what == "wait_recv":
                copy(step).wait_recv()
            else:
                copy(step).wait_send()
            return 0

        lax.fori_loop(1, 16, one, 0)

    z_copy(0).start()
    z_copy(1).start()
    for k in range(4):
        f_copy(k).start()
    each(b_copy, "start")
    for way in (2, 1, 3):
        x_copy(0, way).start()
    each(l_copy, "start")
    hs_copy(0).start()
    s_start(0)
    b_recv[r] = b_send[...]
    l_recv[r] = l_send[r]
    loads[7].wait()

    for index in (1, 2):
        a_in(4 * index).wait_recv()
        s_start(index)
        sib_copy(4 * index).start()
    a_in(12, 0).wait_recv()
    a_in(12, 1).wait_recv()
    s_start(3)
    sib_copy(12).start()
    for k in (1, 3, 2):
        h_in(0, k).wait_recv()
        hs_copy(k).start()
    h_in(1, 0).wait_recv()
    for to in (2, 1, 3):
        x_copy(1, to).start()

    def wait_b(step, _):
        b_copy(step).wait_recv()
        return 0

    lax.fori_loop(1, 16, wait_b, 0)
    b_f32[...] = b_recv[...].reshape(512, 128).astype(F32)
    for h in range(4):
        b_query[:, 128 * h : 128 * h + 128] = (SCALE * b_f32[pl.ds(h, 64, stride=8), :]).astype(BF16)
    bk_all = SCALE * b_f32[pl.ds(4, 64, stride=8), :]
    bv_all = SCALE * b_f32[pl.ds(5, 64, stride=8), :]
    both = bk_all + pltpu.roll(bv_all, 32, 1)
    w_send[...] = (both[0:32] + pltpu.roll(both[32:64], 64, 1)).astype(BF16)
    w_recv[t] = w_send[...]

    acc_q[...] = jnp.zeros_like(acc_q)
    acc_kv[...] = jnp.zeros_like(acc_kv)
    for load in loads[2:5]:
        load.wait()

    def merge(at, half):
        start = pl.multiple_of(at * 512 + half * 256, 256)
        down = a_buf[at, half]
        low = lax.dot_general(
            down, b_query[...], (((0,), (0,)), ((), ())), preferred_element_type=F32
        )
        rows = pl.ds(start, 256)
        wq[rows, :] = (wq[rows, :].astype(F32) + low).astype(BF16)

    def project(part):
        start = pl.multiple_of(part * 2048, 2048)
        states = h_buf[:, :, pl.ds(start, 2048)].reshape(64, 2048)
        acc_q[...] += jnp.dot(states, wq[pl.ds(start, 2048), :], preferred_element_type=F32)
        acc_kv[...] += lax.dot_general(
            states, wkv[:, pl.ds(start, 2048)], (((1,), (1,)), ((), ())), preferred_element_type=F32
        )

    def slot_at(at):
        phase, m = at // 4, at % 4
        middle = ((phase + 1) // 2) % 2
        return middle * (8 * (phase - 1) + 4 * (m // 2) + 1 + m % 2) + (1 - middle) * (4 * m + phase)

    def first(at, _):
        merge(origin(c, slot_at(at)), c)
        return 0

    lax.fori_loop(0, LAG, first, 0)
    h_in(2, 0).wait_recv()
    for to in (2, 1, 3):
        x_copy(2, to).start()
    hs_copy(4).start()

    each(l_copy, "wait_recv")
    slices = l_recv[...].reshape(256, 128)
    block_of = (lax.broadcasted_iota(jnp.int32, (256, 128), 0) // 4) % 4
    sums = jnp.zeros((256, 128), F32)
    for block in range(4):
        sums += lax.dot_general(
            jnp.where(block_of == block, slices, jnp.zeros_like(slices)),
            a_kv[:, 128 * block : 128 * block + 128],
            (((1,), (1,)), ((), ())), preferred_element_type=F32,
        )
    sums = sums.reshape(16, 2, 8, 128)
    p_send[...] = sums[:, 0] + sums[:, 1]
    each(p_copy, "start")
    p_recv[r] = p_send[r]

    def turn(at, _):
        slot = slot_at(at)

        @pl.when((at > 3) & (at < 12))
        def _():
            a_in(slot).wait_recv()
            sib_copy(slot).start()

        @pl.when(at >= 12)
        def _():
            a_in(slot, 0).wait_recv()
            a_in(slot, 1).wait_recv()
            sib_copy(slot).start()

        @pl.when(at == ES)
        def _():
            for k in range(4):
                hs_in(k).wait_recv()
            for k in range(2):
                arrange(2 * zh + k)

        @pl.when(at == EW)
        def _():
            each(w_copy, "start")

        @pl.when(at == EH)
        def _():
            for k in (1, 3, 2):
                h_in(1, k).wait_recv()
                h_in(2, k).wait_recv()
                hs_copy(4 + k).start()

        late = slot_at(at - LAG)

        @pl.when(at > LAG)
        def _():
            sib_in(late).wait_recv()

        merge(origin(c, slot), c)
        merge(origin(other, late), other)
        return 0

    lax.fori_loop(LAG, 16, turn, 0)

    def last(at, _):
        sib_in(slot_at(at)).wait_recv()
        merge(origin(other, slot_at(at)), other)
        return 0

    lax.fori_loop(16 - LAG, 16, last, 0)
    for k in range(4, 8):
        hs_in(k).wait_recv()
    for k in range(2):
        arrange(2 * (1 - zh) + k)

    def project_turn(part, _):
        project(part)
        return 0

    lax.fori_loop(0, 4, project_turn, 0)
    acc = acc_q[...]
    kv = jnp.concatenate([acc_kv[...], jnp.zeros((64, 64), F32)], 1)
    lane = lax.broadcasted_iota(jnp.int32, (64, 128), 1)
    mine = lane // 32 == t % 4
    own_key = jnp.where(mine, pltpu.roll(kv, (t % 4) * 32, 1), 0.0)
    own_value = jnp.where(mine, pltpu.roll(kv, (t % 4) * 32 + 96, 1), 0.0)
    for to in range(16):
        base = 4 * to
        for h in range(4):
            q_f32[to, 4 * h : 4 * h + 4, :] = acc[base : base + 4, 128 * h : 128 * h + 128]
        n_send[to, 0:4, :] = own_key[base : base + 4]
        n_send[to, 4:8, :] = own_value[base : base + 4]
    q_send[...] = q_f32[...].astype(BF16)

    def q_copy(step):
        to = (t + step) % 16
        return remote(q_send.at[to], q_recv.at[t], q_ssem.at[step], q_rsem.at[step], (r, to))

    def n_copy(step):
        to = (t + step) % 16
        return remote(n_send.at[to], n_recv.at[t], n_ssem.at[step], n_rsem.at[step], (r, to))

    def start_q(step, _):
        q_copy(step).start()
        n_copy(step).start()
        return 0

    lax.fori_loop(1, 16, start_q, 0)
    q_recv[t] = q_send[t]
    n_recv[t] = n_send[t]
    loads[5].wait()
    loads[6].wait()

    each(b_copy, "wait_send")
    each(sib_copy, "wait_send")
    each(l_copy, "wait_send")
    each(p_copy, "wait_send")
    each(w_copy, "wait_send")
    for half in range(2):
        z_copy(half).wait_send()
    for slot in range(8):
        hs_copy(slot).wait_send()
    for part in range(3):
        for way in range(1, 4):
            x_copy(part, way).wait_send()
    for k in range(4):
        f_copy(k).wait_send()
        for way in range(2):
            s_copy(k, way).wait_send()
            far_copy(k, way).wait_send()

    each(p_copy, "wait_recv")
    each(w_copy, "wait_recv")
    total = jnp.sum(p_recv[...], 0)
    total = total + pltpu.roll(total, 4, 0)
    total_high = total.astype(BF16).astype(F32)
    total_rest = total - total_high
    key_rank = lax.broadcasted_iota(jnp.int32, (8, 128), 1) < 64
    totals = jnp.concatenate(
        [
            jnp.where(key_rank, total_high, 0.0),
            jnp.where(key_rank, total_rest, 0.0),
            jnp.where(key_rank, 0.0, total_high),
            jnp.where(key_rank, 0.0, total_rest),
        ],
        0,
    ).astype(BF16)
    key_row = lax.broadcasted_iota(jnp.int32, (8, 128), 0) < 4
    quarter = lax.broadcasted_iota(jnp.int32, (32, 128), 1) // 32
    for g in range(4):
        ups = [jnp.zeros((32, 128), F32) for _ in range(4)]
        for u in range(4):
            block = w_recv[4 * g + u].astype(F32)
            for at, held_at in enumerate((0, 2, 1, 3)):
                shift = (32 * u - 32 * held_at) % 128
                moved = pltpu.roll(block, shift, 1) if shift else block
                ups[at] += jnp.where(quarter == u, moved, 0.0)
        up_all = jnp.concatenate(ups, 0).astype(BF16)
        low = jnp.dot(totals, up_all, preferred_element_type=F32)
        low_f32[g] = jnp.where(key_row, low[0:8] + low[8:16], low[16:24] + low[24:32])

    def wait_q(g, u, _):
        step = (t + 16 - 4 * g - u) % 16

        @pl.when(step != 0)
        def _():
            q_copy(step).wait_recv()
            n_copy(step).wait_recv()

        return 0


    cosine, sine = tables[0], tables[1]
    length = length_in[0]
    column = lax.broadcasted_iota(jnp.int32, (64, KEYS), 1)
    step_of = lax.broadcasted_iota(jnp.int32, (64, KEYS), 0) % 4
    valid = (column < length) | ((column >= SLOTS) & (column - SLOTS <= step_of))
    scaling = 1.0 / math.sqrt(HEAD_DIM)

    def rotated(values, cos_rows, sin_rows):
        return values * cos_rows + pltpu.roll(values, 64, values.ndim - 1) * sin_rows

    def o_copy(step):
        to = (t + step) % 16
        return remote(o_send.at[to], o_recv.at[t], o_ssem.at[step], o_rsem.at[step], (r, to))

    def start_o(g, u, _):
        step = (4 * g + u + 16 - t) % 16

        @pl.when(step != 0)
        def _():
            o_copy(step).start()

        return 0

    for g in range(4):
        lax.fori_loop(0, 4, functools.partial(wait_q, g), 0)
        cols = slice(128 * g, 128 * g + 128)
        fresh = n_recv[4 * g] + n_recv[4 * g + 1] + n_recv[4 * g + 2] + n_recv[4 * g + 3]
        fresh = (fresh + low_f32[g]).astype(BF16)
        fresh_key = rotated(fresh.astype(F32), cosine[0:8], sine[0:8])[0:4].astype(BF16)
        fresh_value = fresh[4:8]
        fresh_ref[0, :, cols] = fresh_key
        fresh_ref[1, :, cols] = fresh_value
        pad = jnp.zeros((12, 128), BF16)
        k_buf[SLOTS : SLOTS + 16, cols] = jnp.concatenate([fresh_key, pad], 0)
        v_buf[SLOTS : SLOTS + 16, cols] = jnp.concatenate([fresh_value, pad], 0)
        query = q_recv[4 * g : 4 * g + 4].astype(F32).reshape(64, 128)
        tables = (jnp.concatenate([cosine] * 4, 0), jnp.concatenate([sine] * 4, 0))
        query = rotated(query, *tables).astype(BF16)
        scores = scaling * lax.dot_general(
            query, k_buf[:, cols], (((1,), (1,)), ((), ())), preferred_element_type=F32
        )
        scores = jnp.where(valid, scores, -1e30)
        highest = jnp.max(scores, -1, keepdims=True)
        weights = jnp.where(valid, jnp.exp(scores - highest), 0.0)
        total = jnp.sum(weights, -1, keepdims=True)
        probs = (weights * (1.0 / total)).astype(BF16)
        blended = jnp.dot(probs, v_buf[:, cols], preferred_element_type=F32).astype(BF16)
        o_send[4 * g : 4 * g + 4] = blended.reshape(4, 16, 128)
        lax.fori_loop(0, 4, functools.partial(start_o, g), 0)

    o_recv[t] = o_send[t]

    def wait_q_sends(step, _):
        q_copy(step).wait_send()
        n_copy(step).wait_send()
        return 0

    lax.fori_loop(1, 16, wait_q_sends, 0)

    def wait_o(step, _):
        o_copy(step).wait_recv()
        return 0

    lax.fori_loop(1, 16, wait_o, 0)
    o_f32[...] = o_recv[...].reshape(256, 128).astype(F32)
    for s in range(STEPS):
        for h in range(4):
            out_ref[s, :, 128 * h : 128 * h + 128] = o_f32[
                pl.ds(4 * h + s, 16, stride=16), :
            ].astype(BF16)

    def wait_last(step, _):
        o_copy(step).wait_send()
        return 0

    lax.fori_loop(1, 16, wait_last, 0)


def shards(
    hidden, w_query, w_key, w_value, a_factors, b_query, b_key, b_value,
    key_cache, value_cache, lengths,
):
    anywhere = pl.BlockSpec(memory_space=pltpu.HBM)
    vmem = pl.BlockSpec(memory_space=pltpu.VMEM)
    dma = pltpu.SemaphoreType.DMA
    attended, fresh = pl.pallas_call(
        body,
        out_shape=(
            pltpu.VMEM((4, 16, 512), BF16),
            pltpu.VMEM((2, 4, 512), BF16),
        ),
        in_specs=[anywhere] * 11,
        out_specs=(vmem, vmem),
        scratch_shapes=[
            pltpu.VMEM((2, 16, 128), F32),
            pltpu.SMEM((1,), jnp.int32),
            pltpu.VMEM((4, WIDTH), BF16),
            pltpu.VMEM((4, 512), BF16),
            pltpu.VMEM((4, 32), BF16),
            pltpu.VMEM((4, 32), BF16),
            pltpu.VMEM((WIDTH, 512), BF16),
            pltpu.VMEM((64, WIDTH), BF16),
            pltpu.VMEM((16, 2, 64, 256), BF16),
            pltpu.VMEM((4, 16, WIDTH), BF16),
            pltpu.VMEM((KEYS, 512), BF16),
            pltpu.VMEM((KEYS, 512), BF16),
            pltpu.VMEM((512, 128), F32),
            pltpu.VMEM((32, 128), BF16),
            pltpu.VMEM((16, 32, 128), BF16),
            pltpu.VMEM((64, 512), BF16),
            pltpu.VMEM((32, 128), BF16),
            pltpu.VMEM((2, 16, 1024), F32),
            pltpu.VMEM((16, 2, 16, 1024), BF16),
            pltpu.VMEM((16, WIDTH), F32),
            pltpu.VMEM((128, 512), BF16),
            pltpu.VMEM((16, 16, 128), F32),
            pltpu.VMEM((16, 16, 128), BF16),
            pltpu.VMEM((16, 16, 128), BF16),
            pltpu.VMEM((16, 8, 128), F32),
            pltpu.VMEM((16, 8, 128), F32),
            pltpu.VMEM((16, 32, 128), BF16),
            pltpu.VMEM((4, 8, 128), F32),
            pltpu.VMEM((64, 512), F32),
            pltpu.VMEM((64, 64), F32),
            pltpu.VMEM((16, 16, 128), F32),
            pltpu.VMEM((16, 16, 128), BF16),
            pltpu.VMEM((16, 16, 128), BF16),
            pltpu.VMEM((16, 8, 128), F32),
            pltpu.VMEM((16, 8, 128), F32),
            pltpu.VMEM((16, 16, 128), BF16),
            pltpu.VMEM((16, 16, 128), BF16),
            pltpu.VMEM((256, 128), F32),
            dma((13,)), dma((16,)), dma((16,)), dma((2,)), dma((6, 4)),
            dma((3, 4)), dma((8,)), dma((8,)),
            dma((4,)), dma((4, 2)), dma((4, 2)), dma((16, 2)), dma((16,)), dma((16,)),
            dma((16,)), dma((16,)), dma((16,)), dma((16,)), dma((16,)), dma((16,)),
            dma((16,)), dma((16,)),
            dma((16,)), dma((16,)), dma((16,)), dma((16,)),
        ],
        compiler_params=pltpu.CompilerParams(
            collective_id=0, has_side_effects=True, vmem_limit_bytes=62 * 1024 * 1024
        ),
    )(
        lengths, hidden[:, 0], w_query, w_key.T, w_value.T,
        jnp.swapaxes(a_factors, 1, 2).reshape(192, 512), b_query, b_key, b_value,
        key_cache[0], value_cache[0],
    )
    return attended, fresh[0][:, None], fresh[1][:, None]


def solution(mesh):
    placed = (
        P(None, ("rep", "tp"), None),
        P(None, "tp"),
        P(None, "tp"),
        P(None, "tp"),
        P(None, "rep", None),
        P("rep", "tp"),
        P("rep", "tp"),
        P("rep", "tp"),
        P(("rep", "tp"), None, None),
        P(("rep", "tp"), None, None),
        P(("rep", "tp")),
    )
    return jax.shard_map(
        shards,
        mesh=mesh,
        in_specs=placed,
        out_specs=(
            P(None, "rep", "tp"),
            P(None, ("rep", "tp"), None),
            P(None, ("rep", "tp"), None),
        ),
        check_vma=False,
    )
```
